256 devices in a mesh: scan: 128 (over y_lo, z, x, core), det: 2 (over y_hi).
Axes of the slice: x: 4, y: 4 (y_hi: 2, y_lo: 2; y = y_hi * 2 + y_lo), z: 8, core: 2. Of those that a mesh axis runs over, the one named last changes fastest.
Arguments:
- frames: bfloat16 [512, 512, 1024], P('scan', None, 'det'), may hold values from -6 to 6
- exposure: float32 [512, 512], P('scan'), may hold values from 0.25 to 4
- dark_counts: int32 [1024, 1024], P('scan', 'det'), may hold values from 0 to 11, as said below
- aberration: float32 [1024], P('det'), may hold values from -3.140625 to 3.140625
- margin_codes: int32 [512, 512, 1024], P('scan', None, 'det'), may hold values from 0 to 2, as said below
Outputs:
- object_spectrum: float32 [2, 512, 512], P(None, 'scan', 'det')
The draws below stay inside these ranges and needn't reach their ends.
Inputs may be any that keep to these rules, and one draw needn't show every extreme that they name: `dark_counts`: whole counts; their mean rises with the frame number. `margin_codes`: 1 marks the left double-margin region, 2 the right one, 0 neither; the code is 0 for every pixel at the frequency with q = 0 and a = 0.
All inputs are finite; a program needn't handle non-finite values.
Results may differ from the reference program's by a relative error of at most 0.008.
Values may be sent and summed in bfloat16 or wider, within the bound.
A program may use at most 64 MiB of HBM per device.

```python
import math
import jax
import jax.numpy as jnp
from jax import lax

NY = 512
NX = 512
PIX = 1024
FRAMES = 1024


def draw_dark_counts(key, part):
    key = jax.random.fold_in(key, 11)
    frame_index = jnp.arange(FRAMES, dtype=jnp.int32)[:, None]
    ceiling = jnp.broadcast_to(4 + 9 * frame_index // FRAMES, (FRAMES, PIX))
    return jax.random.randint(key, (FRAMES, PIX), 0, ceiling, dtype=jnp.int32)


def draw_margin_codes(key, part):
    key = jax.random.fold_in(key, 23)
    region_codes = jax.random.randint(key, (NX, NY, PIX), 0, 3, dtype=jnp.int32)
    freq_x = jnp.arange(NX, dtype=jnp.int32)[:, None, None]
    freq_y = jnp.arange(NY, dtype=jnp.int32)[None, :, None]
    return jnp.where((freq_x == 0) & (freq_y == 0), 0, region_codes).astype(jnp.int32)


def steps_of(key, shape, cuts, low, largest):
    loudness = 1.0
    for dim, shards_of in cuts:
        steps = jax.random.uniform(jax.random.fold_in(jax.random.fold_in(key, 6), dim), (shards_of,), jnp.float32, low / len(cuts), largest / len(cuts))
        loudness = loudness * jnp.repeat(jnp.exp(steps), shape[dim] // shards_of).reshape((-1,) + (1,) * (len(shape) - 1 - dim))
    return loudness


def gaussian(rng, extent, width, bound, split=(), held_as=jnp.bfloat16):
    factor_of = steps_of(rng, extent, split, -0.22, 0.18) if split else 1.0
    result = jax.random.normal(rng, extent, jnp.float32) * width * factor_of
    return jnp.minimum(jnp.maximum(result, -bound), bound).astype(held_as)


def setup_inputs(seed: int = 0) -> dict:
    streams_of = jax.random.split(jax.random.key(seed), 6)
    return {
        "frames": gaussian(streams_of[0], (NY, NX, PIX), 1.0, 6.0, ((0, 128), (2, 2))),
        "exposure": jnp.clip(jnp.exp(math.log(4.0) - 2.7725887 * jax.random.uniform(streams_of[1], (NY, NX), jnp.float32) ** steps_of(streams_of[1], (NY, NX), ((0, 128),), -0.2, 0.2)), 0.25, 4.0),
        "dark_counts": draw_dark_counts(jax.random.fold_in(streams_of[5], 71), 0),
        "aberration": jnp.clip(jax.random.uniform(streams_of[3], (PIX,), jnp.float32, -3.140625, 3.140625), -3.140625, 3.140625),
        "margin_codes": draw_margin_codes(jax.random.fold_in(streams_of[5], 71), 0),
    }


def dft_tables(length):
    index_row = jnp.arange(length, dtype=jnp.int32)
    phase_table = 2.0 * math.pi / length * (index_row[:, None] * index_row[None, :] % length).astype(jnp.float32)
    norm_scale = 1.0 / math.sqrt(length)
    return ((jnp.cos(phase_table) * norm_scale).astype(jnp.bfloat16), (-jnp.sin(phase_table) * norm_scale).astype(jnp.bfloat16))

def reference(frames, exposure, dark_counts, aberration, margin_codes):
    dark_mean = lax.optimization_barrier(jnp.sum(dark_counts.astype(jnp.float32), axis=0)) / FRAMES
    cos_x, sin_x = dft_tables(NX)
    cos_y, sin_y = dft_tables(NY)
    cos_xf = cos_x.astype(jnp.float32)
    sin_xf = sin_x.astype(jnp.float32)
    cos_yf = cos_y.astype(jnp.float32)
    sin_yf = sin_y.astype(jnp.float32)
    block_size = 64 if PIX % 64 == 0 else PIX
    count_blocks = PIX // block_size

    def one_block(offset_start):
        raw_block = lax.dynamic_slice_in_dim(frames, offset_start, block_size, 2)
        dark_part = lax.dynamic_slice_in_dim(dark_mean, offset_start, block_size, 0)
        corrected = (raw_block.astype(jnp.float32) - exposure[:, :, None] * dark_part[None, None, :]).astype(jnp.bfloat16)
        corrected_f = corrected.astype(jnp.float32)
        spectra_real = jnp.einsum('yxp,xq->yqp', corrected_f, cos_xf).astype(jnp.bfloat16).astype(jnp.float32)
        spectra_imag = jnp.einsum('yxp,xq->yqp', corrected_f, sin_xf).astype(jnp.bfloat16).astype(jnp.float32)
        full_real = jnp.einsum('ay,yqp->qap', cos_yf, spectra_real) - jnp.einsum('ay,yqp->qap', sin_yf, spectra_imag)
        full_imag = jnp.einsum('ay,yqp->qap', cos_yf, spectra_imag) + jnp.einsum('ay,yqp->qap', sin_yf, spectra_real)
        region_part = lax.dynamic_slice_in_dim(margin_codes, offset_start, block_size, 2)
        weight = (region_part == 1).astype(jnp.float32) - (region_part == 2).astype(jnp.float32)
        angle_part = lax.dynamic_slice_in_dim(aberration, offset_start, block_size, 0)
        phase_cos = jnp.cos(angle_part)
        phase_sin = jnp.sin(angle_part)
        part_real = lax.optimization_barrier(jnp.sum(weight * (full_real * phase_cos + full_imag * phase_sin), axis=2))
        part_imag = lax.optimization_barrier(jnp.sum(weight * (full_imag * phase_cos - full_real * phase_sin), axis=2))
        return jnp.stack([part_real, part_imag])
    starts = jnp.arange(count_blocks, dtype=jnp.int32) * block_size
    partial_value = lax.map(one_block, starts)
    return lax.optimization_barrier(jnp.sum(partial_value, axis=0)) / math.sqrt(PIX)
```

```python
import functools
import math

import jax
import jax.numpy as jnp
import ml_dtypes
import numpy as np
from jax import lax
from jax.experimental import pallas as pl
from jax.experimental.pallas import tpu as pltpu
from jax.sharding import PartitionSpec as P

MESH = pl.DeviceIdType.MESH
LANES = 128
NEAR = 8


def dft_tables(length):
    index_row = np.arange(length, dtype=np.int64)
    products = (index_row[:, None] * index_row[None, :] % length).astype(np.float32)
    phase = np.float32(2.0 * math.pi / length) * products
    scale = np.float32(1.0 / math.sqrt(length))
    return (
        (np.cos(phase) * scale).astype(ml_dtypes.bfloat16),
        (-np.sin(phase) * scale).astype(ml_dtypes.bfloat16),
    )


def row_table(length):
    cos, sin = dft_tables(length)
    return np.stack([cos.T, sin.T], axis=1).reshape(2 * length, length)


def column_table(length, rows, tile):
    cos, sin = dft_tables(length)
    real = np.stack([cos, -sin], axis=1)
    imag = np.stack([sin, cos], axis=1)
    both = np.stack([real, imag]).reshape(2, length, 2, length // rows, rows)
    both = both.transpose(0, 1, 3, 2, 4).reshape(2, length // tile, tile, 2 * length)
    return np.ascontiguousarray(both.transpose(1, 0, 2, 3)).reshape(
        length // tile, 2 * tile, 2 * length
    )


def kernel(
    n, rows, chunks, tile, frame_total, scale,
    frames, exposure, dark, aberration, codes, row_tab, col_tab, out,
    frames_v, codes_v, row_v, col_v, spread, corrected, wide, send, recv, gathered, acc,
    near_buf, far_buf, dark_row, turn, halves, half_in,
    load_sem, near_sem, far_sem, send_sem, recv_sem, det_sem,
):
    me = lax.axis_index("scan")
    det = lax.axis_index("det")
    nx = frames_v.shape[2]
    q_rows = 2 * rows * rows
    far = n // NEAR

    loads = [pltpu.make_async_copy(row_tab, row_v, load_sem.at[0])]
    loads += [
        pltpu.make_async_copy(
            frames.at[:, :, pl.ds(c * LANES, LANES)], frames_v.at[c], load_sem.at[1 + c]
        )
        for c in range(chunks)
    ]
    loads.append(pltpu.make_async_copy(col_tab, col_v, load_sem.at[1 + chunks]))
    code_loads = [
        pltpu.make_async_copy(
            codes.at[:, :, pl.ds(c * LANES, LANES)], codes_v.at[c], load_sem.at[2 + chunks + c]
        )
        for c in range(chunks)
    ]
    for load in loads + code_loads:
        load.start()

    barrier = pltpu.get_barrier_semaphore()

    def greet(j, carry):
        pl.semaphore_signal(
            barrier, inc=1, device_id={"scan": lax.rem(me + j, n)}, device_id_type=MESH
        )
        return carry

    lax.fori_loop(1, n, greet, 0)
    pl.semaphore_signal(barrier, inc=1, device_id={"det": 1 - det}, device_id_type=MESH)

    position = lax.rem(me, NEAR)
    group = me // NEAR
    local_sum = jnp.sum(dark[...].astype(jnp.float32), axis=0, keepdims=True)
    near_buf[position] = local_sum
    turned = jnp.concatenate([exposure[...], jnp.zeros_like(exposure[...])], axis=0).T
    for y in range(rows):
        spread[y] = jnp.broadcast_to(turned[:, y : y + 1], (nx, LANES))
    angle = jnp.broadcast_to(aberration[...], (8, aberration.shape[1]))
    cos, sin = jnp.cos(angle), jnp.sin(angle)
    for c in range(chunks):
        turn[c, 0] = cos[:, c * LANES : (c + 1) * LANES]
        turn[c, 1] = sin[:, c * LANES : (c + 1) * LANES]
    acc[...] = jnp.zeros_like(acc)

    pl.semaphore_wait(barrier, n)

    def send_near(j, carry):
        peer = group * NEAR + lax.rem(position + j, NEAR)
        pltpu.make_async_remote_copy(
            src_ref=near_buf.at[position], dst_ref=near_buf.at[position],
            send_sem=near_sem.at[0], recv_sem=near_sem.at[1],
            device_id={"scan": peer}, device_id_type=MESH,
        ).start()
        return carry

    lax.fori_loop(1, NEAR, send_near, 0)
    some = near_buf.at[pl.ds(0, NEAR - 1)]
    pltpu.make_async_copy(some, some, near_sem.at[1]).wait()
    far_buf[group] = jnp.sum(near_buf[...], axis=0)

    def send_far(j, carry):
        peer = lax.rem(group + j, far) * NEAR + position
        pltpu.make_async_remote_copy(
            src_ref=far_buf.at[group], dst_ref=far_buf.at[group],
            send_sem=far_sem.at[0], recv_sem=far_sem.at[1],
            device_id={"scan": peer}, device_id_type=MESH,
        ).start()
        return carry

    lax.fori_loop(1, far, send_far, 0)
    most = far_buf.at[pl.ds(0, far - 1)]
    pltpu.make_async_copy(most, most, far_sem.at[1]).wait()
    mean = jnp.sum(far_buf[...], axis=0) / frame_total
    for c in range(chunks):
        dark_row[c] = jnp.broadcast_to(mean[:, c * LANES : (c + 1) * LANES], (8, LANES))

    loads[0].wait()
    m_tile = 512

    def spectra(c, carry):
        pltpu.make_async_copy(frames_v.at[c], frames_v.at[c], load_sem.at[1 + c]).wait()
        level = jnp.broadcast_to(dark_row[c, 0:1], (nx, LANES))
        for y in range(rows):
            value = frames_v[c, y].astype(jnp.float32) - spread[y] * level
            corrected[:, y * LANES : (y + 1) * LANES] = value.astype(jnp.bfloat16)
        for m in range(2 * nx // m_tile):
            part = jnp.dot(
                row_v[m * m_tile : (m + 1) * m_tile], corrected[...],
                preferred_element_type=jnp.float32,
            )
            for y in range(rows):
                wide[pl.ds(m * m_tile * rows + y, m_tile, stride=rows), :] = part[
                    :, y * LANES : (y + 1) * LANES
                ]

        def narrow(i, carry):
            at = pl.multiple_of(i * 512, 512)
            send[c, pl.ds(at, 512)] = wide[pl.ds(at, 512)].astype(jnp.bfloat16)
            return carry

        lax.fori_loop(0, n * q_rows // 512, narrow, 0)

        def ship(j, carry):
            peer = lax.rem(me + j, n)
            pltpu.make_async_remote_copy(
                src_ref=send.at[c, pl.ds(pl.multiple_of(peer * q_rows, q_rows), q_rows)],
                dst_ref=recv.at[c, pl.ds(pl.multiple_of(me * q_rows, q_rows), q_rows)],
                send_sem=send_sem, recv_sem=recv_sem.at[c],
                device_id={"scan": peer}, device_id_type=MESH,
            ).start()
            return carry

        lax.fori_loop(1, n, ship, 0)
        mine = pl.ds(pl.multiple_of(me * q_rows, q_rows), q_rows)
        recv[c, mine] = send[c, mine]
        return carry

    lax.fori_loop(0, chunks, spectra, 0)

    loads[1 + chunks].wait()

    def weigh(c, carry):
        pltpu.make_async_copy(codes_v.at[c], codes_v.at[c], load_sem.at[2 + chunks + c]).wait()
        others = recv.at[c, pl.ds(0, (n - 1) * q_rows)]
        pltpu.make_async_copy(others, others, recv_sem.at[c]).wait()

        def regroup(s, carry):
            at = pl.multiple_of(s * 2 * q_rows, 2 * q_rows)
            block = recv[c, pl.ds(at, 2 * q_rows)].astype(jnp.float32)
            unit = 2 * rows
            to = pl.ds(pl.multiple_of(s * 2 * unit, 2 * unit), 2 * unit)
            for q in range(rows):
                pair = jnp.concatenate(
                    [
                        block[q * unit : (q + 1) * unit],
                        block[q_rows + q * unit : q_rows + (q + 1) * unit],
                    ],
                    axis=0,
                )
                gathered[to, q * LANES : (q + 1) * LANES] = pair.astype(jnp.bfloat16)
            return carry

        lax.fori_loop(0, n // 2, regroup, 0, unroll=4)
        cos = jnp.broadcast_to(turn[c, 0, 0:1], (tile, LANES))
        sin = jnp.broadcast_to(turn[c, 1, 0:1], (tile, LANES))

        def column(t, carry):
            full = jnp.dot(col_v[t], gathered[...], preferred_element_type=jnp.float32)
            at = pl.ds(pl.multiple_of(t * tile, tile), tile)
            for q in range(rows):
                real = full[:tile, q * LANES : (q + 1) * LANES]
                imag = full[tile:, q * LANES : (q + 1) * LANES]
                code = codes_v[c, q, at]
                weight = (code == 1).astype(jnp.float32) - (code == 2).astype(jnp.float32)
                acc[q, at] += weight * (real * cos + imag * sin)
                acc[rows + q, at] += weight * (imag * cos - real * sin)
            return carry

        lax.fori_loop(0, col_v.shape[0], column, 0)
        return carry

    lax.fori_loop(0, chunks, weigh, 0)

    row = lax.broadcasted_iota(jnp.int32, (2 * rows, LANES), 0)
    total = jnp.zeros((2 * rows, acc.shape[1]), jnp.float32)
    for i in range(2 * rows):
        pick = (row == i).astype(jnp.bfloat16)
        value = acc[i]
        for _ in range(3):
            high = value.astype(jnp.bfloat16)
            total += lax.dot_general(
                pick, high, (((1,), (1,)), ((), ())), preferred_element_type=jnp.float32
            )
            value = value - high.astype(jnp.float32)
    total = total / scale
    width = half_in.shape[1]
    halves[0] = total[:, :width]
    halves[1] = total[:, width:]
    swap = pltpu.make_async_remote_copy(
        src_ref=halves.at[1 - det], dst_ref=half_in, send_sem=det_sem.at[0],
        recv_sem=det_sem.at[1], device_id={"det": 1 - det}, device_id_type=MESH,
    )
    swap.start()
    swap.wait()
    result = halves[det] + half_in[...]
    out[0] = result[:rows]
    out[1] = result[rows:]

    pltpu.make_async_copy(some, some, near_sem.at[0]).wait()
    pltpu.make_async_copy(most, most, far_sem.at[0]).wait()
    sent = send.at[:, pl.ds(0, (n - 1) * q_rows)]
    pltpu.make_async_copy(sent, sent, send_sem).wait()


def solution(mesh):
    n = mesh.shape["scan"]

    def on_device(frames, exposure, dark_counts, aberration, margin_codes):
        rows, nx, pix = frames.shape
        ny = rows * n
        chunks = pix // LANES
        tile = 256
        row_tab = row_table(nx)
        col_tab = column_table(ny, rows, tile)
        hbm = pl.BlockSpec(memory_space=pl.ANY)
        vmem = pl.BlockSpec(memory_space=pltpu.VMEM)
        body = functools.partial(
            kernel, n, rows, chunks, tile, dark_counts.shape[0] * n,
            math.sqrt(pix * mesh.shape["det"]),
        )
        message_rows = 2 * rows * ny
        return pl.pallas_call(
            body,
            out_shape=jax.ShapeDtypeStruct((2, rows, ny // mesh.shape["det"]), jnp.float32),
            in_specs=[hbm, vmem, vmem, vmem, hbm, hbm, hbm],
            out_specs=vmem,
            scratch_shapes=[
                pltpu.VMEM((chunks, rows, nx, LANES), jnp.bfloat16),
                pltpu.VMEM((chunks, rows, ny, LANES), jnp.int32),
                pltpu.VMEM(row_tab.shape, jnp.bfloat16),
                pltpu.VMEM(col_tab.shape, jnp.bfloat16),
                pltpu.VMEM((rows, nx, LANES), jnp.float32),
                pltpu.VMEM((nx, rows * LANES), jnp.bfloat16),
                pltpu.VMEM((message_rows, LANES), jnp.float32),
                pltpu.VMEM((chunks, message_rows, LANES), jnp.bfloat16),
                pltpu.VMEM((chunks, message_rows, LANES), jnp.bfloat16),
                pltpu.VMEM((2 * ny, rows * LANES), jnp.bfloat16),
                pltpu.VMEM((2 * rows, ny, LANES), jnp.float32),
                pltpu.VMEM((NEAR, 1, pix), jnp.float32),
                pltpu.VMEM((n // NEAR, 1, pix), jnp.float32),
                pltpu.VMEM((chunks, 8, LANES), jnp.float32),
                pltpu.VMEM((chunks, 2, 8, LANES), jnp.float32),
                pltpu.VMEM((2, 2 * rows, ny // 2), jnp.float32),
                pltpu.VMEM((2 * rows, ny // 2), jnp.float32),
                pltpu.SemaphoreType.DMA((2 + 2 * chunks,)),
                pltpu.SemaphoreType.DMA((2,)),
                pltpu.SemaphoreType.DMA((2,)),
                pltpu.SemaphoreType.DMA,
                pltpu.SemaphoreType.DMA((chunks,)),
                pltpu.SemaphoreType.DMA((2,)),
            ],
            compiler_params=pltpu.CompilerParams(
                collective_id=0, has_side_effects=True, vmem_limit_bytes=52 * 1024 * 1024
            ),
        )(
            frames, exposure, dark_counts, aberration.reshape(1, pix), margin_codes,
            jnp.asarray(row_tab), jnp.asarray(col_tab),
        )

    placed = (
        P("scan", None, "det"),
        P("scan", None),
        P("scan", "det"),
        P("det"),
        P("scan", None, "det"),
    )
    return jax.shard_map(
        on_device, mesh=mesh, in_specs=placed, out_specs=P(None, "scan", "det"), check_vma=False
    )
```

```python
import functools
import math

import jax
import jax.numpy as jnp
import ml_dtypes
import numpy as np
from jax import lax
from jax.experimental import pallas as pl
from jax.experimental.pallas import tpu as pltpu
from jax.sharding import PartitionSpec as P

MESH = pl.DeviceIdType.MESH
LANES = 128
NEAR = 8


def dft_tables(length):
    index_row = np.arange(length, dtype=np.int64)
    products = (index_row[:, None] * index_row[None, :] % length).astype(np.float32)
    phase = np.float32(2.0 * math.pi / length) * products
    scale = np.float32(1.0 / math.sqrt(length))
    return (
        (np.cos(phase) * scale).astype(ml_dtypes.bfloat16),
        (-np.sin(phase) * scale).astype(ml_dtypes.bfloat16),
    )


def row_table(length):
    cos, sin = dft_tables(length)
    return np.stack([cos.T, sin.T], axis=1).reshape(2 * length, length)


def column_table(length, rows, tile):
    cos, sin = dft_tables(length)
    real = np.stack([cos, -sin], axis=1)
    imag = np.stack([sin, cos], axis=1)
    both = np.stack([real, imag]).reshape(2, length, 2, length // rows, rows)
    both = both.transpose(0, 1, 3, 2, 4).reshape(2, length // tile, tile, 2 * length)
    return np.ascontiguousarray(both.transpose(1, 0, 2, 3)).reshape(
        length // tile, 2 * tile, 2 * length
    )


def kernel(
    n, rows, chunks, tile, frame_total, scale,
    frames, exposure_h, dark_h, aberration_h, codes, row_tab, col_tab, out,
    exposure, dark, aberration,
    frames_v, codes_v, row_v, col_v, joined, wide, level, send, recv, gathered, acc,
    near_buf, far_buf, dark_row, turn, level_out, level_in, halves, half_in,
    small_sem, load_sem, near_sem, far_sem, level_sem, send_sem, recv_sem, det_sem,
):
    me = lax.axis_index("scan")
    det = lax.axis_index("det")
    nx = frames_v.shape[2]
    q_rows = 2 * rows * rows
    far = n // NEAR

    barrier = pltpu.get_barrier_semaphore()

    def greet(j, carry):
        pl.semaphore_signal(
            barrier, inc=1, device_id={"scan": lax.rem(me + j, n)}, device_id_type=MESH
        )
        return carry

    lax.fori_loop(1, n, greet, 0)
    pl.semaphore_signal(barrier, inc=1, device_id={"det": 1 - det}, device_id_type=MESH)

    small = [
        pltpu.make_async_copy(dark_h, dark, small_sem.at[0]),
        pltpu.make_async_copy(exposure_h, exposure, small_sem.at[1]),
        pltpu.make_async_copy(aberration_h, aberration, small_sem.at[2]),
    ]
    loads = [pltpu.make_async_copy(row_tab, row_v, load_sem.at[0])]
    loads += [
        pltpu.make_async_copy(
            frames.at[:, :, pl.ds(c * LANES, LANES)], frames_v.at[c], load_sem.at[1 + c]
        )
        for c in range(chunks)
    ]
    loads.append(pltpu.make_async_copy(col_tab, col_v, load_sem.at[1 + chunks]))
    code_loads = [
        pltpu.make_async_copy(
            codes.at[:, :, pl.ds(c * LANES, LANES)], codes_v.at[c], load_sem.at[2 + chunks + c]
        )
        for c in range(chunks)
    ]
    for load in small + loads + code_loads:
        load.start()

    position = lax.rem(me, NEAR)
    group = me // NEAR
    small[0].wait()
    near_buf[position] = jnp.sum(dark[...].astype(jnp.float32), axis=0, keepdims=True)
    loads[0].wait()
    m_tile = 512

    def spectra(c):
        loads[1 + c].wait()
        for y in range(rows):
            joined[:, y * LANES : (y + 1) * LANES] = frames_v[c, y]
        for m in range(2 * nx // m_tile):
            part = jnp.dot(
                row_v[m * m_tile : (m + 1) * m_tile], joined[...],
                preferred_element_type=jnp.float32,
            )
            for y in range(rows):
                wide[pl.ds(m * m_tile * rows + y, m_tile, stride=rows), :] = part[
                    :, y * LANES : (y + 1) * LANES
                ]

        def narrow(i, carry):
            at = pl.multiple_of(i * 512, 512)
            send[c, pl.ds(at, 512)] = wide[pl.ds(at, 512)].astype(jnp.bfloat16)
            return carry

        lax.fori_loop(0, n * q_rows // 512, narrow, 0)
        mine = pl.ds(pl.multiple_of(me * q_rows, q_rows), q_rows)
        recv[c, mine] = send[c, mine]

    def ship(c):
        def one(j, carry):
            peer = lax.rem(me + j, n)
            pltpu.make_async_remote_copy(
                src_ref=send.at[c, pl.ds(pl.multiple_of(peer * q_rows, q_rows), q_rows)],
                dst_ref=recv.at[c, pl.ds(pl.multiple_of(me * q_rows, q_rows), q_rows)],
                send_sem=send_sem, recv_sem=recv_sem.at[c],
                device_id={"scan": peer}, device_id_type=MESH,
            ).start()
            return carry

        lax.fori_loop(1, n, one, 0)

    spectra(0)
    pl.semaphore_wait(barrier, n)

    def send_near(j, carry):
        peer = group * NEAR + lax.rem(position + j, NEAR)
        pltpu.make_async_remote_copy(
            src_ref=near_buf.at[position], dst_ref=near_buf.at[position],
            send_sem=near_sem.at[0], recv_sem=near_sem.at[1],
            device_id={"scan": peer}, device_id_type=MESH,
        ).start()
        return carry

    lax.fori_loop(1, NEAR, send_near, 0)
    ship(0)
    spectra(1)
    ship(1)

    small[1].wait()
    turned = jnp.concatenate([exposure[...], jnp.zeros_like(exposure[...])], axis=0).T
    for y in range(rows):
        rest = jnp.broadcast_to(turned[:, y : y + 1], (nx, LANES))
        total = jnp.zeros((2 * nx, LANES), jnp.float32)
        for _ in range(3):
            high = rest.astype(jnp.bfloat16)
            total += jnp.dot(row_v[...], high, preferred_element_type=jnp.float32)
            rest = rest - high.astype(jnp.float32)
        level[pl.ds(y, 2 * nx, stride=rows), :] = total
    per_row = LANES // q_rows
    diagonal = lax.broadcasted_iota(jnp.int32, (LANES, LANES), 0) == lax.broadcasted_iota(
        jnp.int32, (LANES, LANES), 1
    )

    def pack(i, carry):
        block = level[pl.ds(pl.multiple_of(i * LANES, LANES), LANES)]
        level_out[i] = jnp.sum(jnp.where(diagonal, block, 0.0), axis=0, keepdims=True)
        return carry

    lax.fori_loop(0, n // per_row, pack, 0)

    def send_level(j, carry):
        peer = lax.rem(me + j, n)
        pltpu.make_async_remote_copy(
            src_ref=level_out.at[peer // per_row], dst_ref=level_in.at[me],
            send_sem=level_sem.at[0], recv_sem=level_sem.at[1],
            device_id={"scan": peer}, device_id_type=MESH,
        ).start()
        return carry

    lax.fori_loop(1, n, send_level, 0)
    level_in[me] = level_out[me // per_row]

    some = near_buf.at[pl.ds(0, NEAR - 1)]
    pltpu.make_async_copy(some, some, near_sem.at[1]).wait()
    far_buf[group] = jnp.sum(near_buf[...], axis=0)

    def send_far(j, carry):
        peer = lax.rem(group + j, far) * NEAR + position
        pltpu.make_async_remote_copy(
            src_ref=far_buf.at[group], dst_ref=far_buf.at[group],
            send_sem=far_sem.at[0], recv_sem=far_sem.at[1],
            device_id={"scan": peer}, device_id_type=MESH,
        ).start()
        return carry

    lax.fori_loop(1, far, send_far, 0)
    for c in range(2, chunks):
        spectra(c)
        ship(c)

    small[2].wait()
    angle = jnp.broadcast_to(aberration[...], (8, aberration.shape[1]))
    cos, sin = jnp.cos(angle), jnp.sin(angle)
    for c in range(chunks):
        turn[c, 0] = cos[:, c * LANES : (c + 1) * LANES]
        turn[c, 1] = sin[:, c * LANES : (c + 1) * LANES]
    acc[...] = jnp.zeros_like(acc)
    levels = level_in.at[pl.ds(0, n - 1)]
    pltpu.make_async_copy(levels, levels, level_sem.at[1]).wait()
    wide[0:n] = level_in[...].reshape(n, LANES).T
    own = wide[pl.ds(pl.multiple_of(lax.rem(me, per_row) * q_rows, q_rows), q_rows)]
    lane = lax.broadcasted_iota(jnp.int32, (q_rows, LANES), 1)

    def unpack(s, carry):
        column = jnp.sum(jnp.where(lane == s, own, 0.0), axis=1, keepdims=True)
        level[pl.ds(pl.multiple_of(s * q_rows, q_rows), q_rows)] = jnp.broadcast_to(
            column, (q_rows, LANES)
        )
        return carry

    lax.fori_loop(0, n, unpack, 0)
    most = far_buf.at[pl.ds(0, far - 1)]
    pltpu.make_async_copy(most, most, far_sem.at[1]).wait()
    mean = jnp.sum(far_buf[...], axis=0) / frame_total
    for c in range(chunks):
        dark_row[c] = jnp.broadcast_to(mean[:, c * LANES : (c + 1) * LANES], (8, LANES))

    loads[1 + chunks].wait()

    def weigh(c, carry):
        pltpu.make_async_copy(codes_v.at[c], codes_v.at[c], load_sem.at[2 + chunks + c]).wait()
        others = recv.at[c, pl.ds(0, (n - 1) * q_rows)]
        pltpu.make_async_copy(others, others, recv_sem.at[c]).wait()

        dark_mean = jnp.broadcast_to(dark_row[c, 0:1], (2 * q_rows, LANES))

        def regroup(s, carry):
            at = pl.multiple_of(s * 2 * q_rows, 2 * q_rows)
            block = recv[c, pl.ds(at, 2 * q_rows)].astype(jnp.float32)
            block = block - level[pl.ds(at, 2 * q_rows)] * dark_mean
            unit = 2 * rows
            to = pl.ds(pl.multiple_of(s * 2 * unit, 2 * unit), 2 * unit)
            for q in range(rows):
                pair = jnp.concatenate(
                    [
                        block[q * unit : (q + 1) * unit],
                        block[q_rows + q * unit : q_rows + (q + 1) * unit],
                    ],
                    axis=0,
                )
                gathered[to, q * LANES : (q + 1) * LANES] = pair.astype(jnp.bfloat16)
            return carry

        lax.fori_loop(0, n // 2, regroup, 0, unroll=4)
        cos = jnp.broadcast_to(turn[c, 0, 0:1], (tile, LANES))
        sin = jnp.broadcast_to(turn[c, 1, 0:1], (tile, LANES))

        def column(t, carry):
            full = jnp.dot(col_v[t], gathered[...], preferred_element_type=jnp.float32)
            at = pl.ds(pl.multiple_of(t * tile, tile), tile)
            for q in range(rows):
                real = full[:tile, q * LANES : (q + 1) * LANES]
                imag = full[tile:, q * LANES : (q + 1) * LANES]
                code = codes_v[c, q, at]
                weight = (code == 1).astype(jnp.float32) - (code == 2).astype(jnp.float32)
                acc[q, at] += weight * (real * cos + imag * sin)
                acc[rows + q, at] += weight * (imag * cos - real * sin)
            return carry

        lax.fori_loop(0, col_v.shape[0], column, 0)
        return carry

    lax.fori_loop(0, chunks, weigh, 0)

    row = lax.broadcasted_iota(jnp.int32, (2 * rows, LANES), 0)
    total = jnp.zeros((2 * rows, acc.shape[1]), jnp.float32)
    for i in range(2 * rows):
        pick = (row == i).astype(jnp.bfloat16)
        value = acc[i]
        for _ in range(2):
            high = value.astype(jnp.bfloat16)
            total += lax.dot_general(
                pick, high, (((1,), (1,)), ((), ())), preferred_element_type=jnp.float32
            )
            value = value - high.astype(jnp.float32)
    total = total / scale
    width = half_in.shape[1]
    halves[0] = total[:, :width]
    halves[1] = total[:, width:]
    swap = pltpu.make_async_remote_copy(
        src_ref=halves.at[1 - det], dst_ref=half_in, send_sem=det_sem.at[0],
        recv_sem=det_sem.at[1], device_id={"det": 1 - det}, device_id_type=MESH,
    )
    swap.start()
    swap.wait()
    result = halves[det] + half_in[...]
    out[0] = result[:rows]
    out[1] = result[rows:]

    pltpu.make_async_copy(some, some, near_sem.at[0]).wait()
    pltpu.make_async_copy(most, most, far_sem.at[0]).wait()
    pltpu.make_async_copy(levels, levels, level_sem.at[0]).wait()
    sent = send.at[:, pl.ds(0, (n - 1) * q_rows)]
    pltpu.make_async_copy(sent, sent, send_sem).wait()


def solution(mesh):
    n = mesh.shape["scan"]

    def on_device(frames, exposure, dark_counts, aberration, margin_codes):
        rows, nx, pix = frames.shape
        ny = rows * n
        chunks = pix // LANES
        tile = 256
        row_tab = row_table(nx)
        col_tab = column_table(ny, rows, tile)
        hbm = pl.BlockSpec(memory_space=pl.ANY)
        vmem = pl.BlockSpec(memory_space=pltpu.VMEM)
        body = functools.partial(
            kernel, n, rows, chunks, tile, dark_counts.shape[0] * n,
            math.sqrt(pix * mesh.shape["det"]),
        )
        message_rows = 2 * rows * ny
        return pl.pallas_call(
            body,
            out_shape=jax.ShapeDtypeStruct((2, rows, ny // mesh.shape["det"]), jnp.float32),
            in_specs=[hbm] * 7,
            out_specs=vmem,
            scratch_shapes=[
                pltpu.VMEM((rows, nx), jnp.float32),
                pltpu.VMEM(dark_counts.shape, jnp.int32),
                pltpu.VMEM((1, pix), jnp.float32),
                pltpu.VMEM((chunks, rows, nx, LANES), jnp.bfloat16),
                pltpu.VMEM((chunks, rows, ny, LANES), jnp.int32),
                pltpu.VMEM(row_tab.shape, jnp.bfloat16),
                pltpu.VMEM(col_tab.shape, jnp.bfloat16),
                pltpu.VMEM((nx, rows * LANES), jnp.bfloat16),
                pltpu.VMEM((message_rows, LANES), jnp.float32),
                pltpu.VMEM((message_rows, LANES), jnp.float32),
                pltpu.VMEM((chunks, message_rows, LANES), jnp.bfloat16),
                pltpu.VMEM((chunks, message_rows, LANES), jnp.bfloat16),
                pltpu.VMEM((2 * ny, rows * LANES), jnp.bfloat16),
                pltpu.VMEM((2 * rows, ny, LANES), jnp.float32),
                pltpu.VMEM((NEAR, 1, pix), jnp.float32),
                pltpu.VMEM((n // NEAR, 1, pix), jnp.float32),
                pltpu.VMEM((chunks, 8, LANES), jnp.float32),
                pltpu.VMEM((chunks, 2, 8, LANES), jnp.float32),
                pltpu.VMEM((n * 2 * rows * rows // LANES, 1, LANES), jnp.float32),
                pltpu.VMEM((n, 1, LANES), jnp.float32),
                pltpu.VMEM((2, 2 * rows, ny // 2), jnp.float32),
                pltpu.VMEM((2 * rows, ny // 2), jnp.float32),
                pltpu.SemaphoreType.DMA((3,)),
                pltpu.SemaphoreType.DMA((2 + 2 * chunks,)),
                pltpu.SemaphoreType.DMA((2,)),
                pltpu.SemaphoreType.DMA((2,)),
                pltpu.SemaphoreType.DMA((2,)),
                pltpu.SemaphoreType.DMA,
                pltpu.SemaphoreType.DMA((chunks,)),
                pltpu.SemaphoreType.DMA((2,)),
            ],
            compiler_params=pltpu.CompilerParams(
                collective_id=0, has_side_effects=True, vmem_limit_bytes=63 * 1024 * 1024
            ),
        )(
            frames, exposure, dark_counts, aberration.reshape(1, pix), margin_codes,
            jnp.asarray(row_tab), jnp.asarray(col_tab),
        )

    placed = (
        P("scan", None, "det"),
        P("scan", None),
        P("scan", "det"),
        P("det"),
        P("scan", None, "det"),
    )
    return jax.shard_map(
        on_device, mesh=mesh, in_specs=placed, out_specs=P(None, "scan", "det"), check_vma=False
    )
```

```python
import functools
import math

import jax
import jax.numpy as jnp
import ml_dtypes
import numpy as np
from jax import lax
from jax.experimental import pallas as pl
from jax.experimental.pallas import tpu as pltpu
from jax.sharding import PartitionSpec as P

MESH = pl.DeviceIdType.MESH
LANES = 128
NEAR = 8


def dft_tables(length):
    index_row = np.arange(length, dtype=np.int64)
    products = (index_row[:, None] * index_row[None, :] % length).astype(np.float32)
    phase = np.float32(2.0 * math.pi / length) * products
    scale = np.float32(1.0 / math.sqrt(length))
    return (
        (np.cos(phase) * scale).astype(ml_dtypes.bfloat16),
        (-np.sin(phase) * scale).astype(ml_dtypes.bfloat16),
    )


def row_table(length):
    cos, sin = dft_tables(length)
    return np.stack([cos.T, sin.T], axis=1).reshape(2 * length, length)


def column_table(length, rows, tile):
    cos, sin = dft_tables(length)
    real = np.stack([cos, -sin], axis=1)
    imag = np.stack([sin, cos], axis=1)
    both = np.stack([real, imag]).reshape(2, length, 2, length // rows, rows)
    both = both.transpose(0, 1, 3, 2, 4).reshape(2, length // tile, tile, 2 * length)
    return np.ascontiguousarray(both.transpose(1, 0, 2, 3)).reshape(
        length // tile, 2 * tile, 2 * length
    )


def kernel(
    n, rows, chunks, tile, frame_total, scale,
    frames, exposure_h, dark_h, aberration_h, codes, row_tab, col_tab, out,
    exposure, dark, aberration,
    frames_v, codes_v, row_v, col_v, joined, wide, level, send, stage, recv, gathered, acc,
    near_buf, far_buf, dark_row, turn, level_out, level_stage, level_pack, level_in, halves, half_in,
    small_sem, load_sem, dark_near_sem, dark_far_sem, level_near_sem, level_far_sem,
    near_send, near_recv, far_send, far_recv, det_sem,
):
    me = lax.axis_index("scan")
    det = lax.axis_index("det")
    nx = frames_v.shape[2]
    unit = 2 * rows
    q_rows = unit * rows
    far = n // NEAR
    position = lax.rem(me, NEAR)
    group = lax.div(me, NEAR)

    def near_peer(j):
        return lax.rem(position + j, NEAR)

    def far_peer(j):
        return lax.rem(group + j, far)

    def at(g, p):
        return {"scan": g * NEAR + p}

    barrier = pltpu.get_barrier_semaphore()
    for j in range(1, far):
        pl.semaphore_signal(
            barrier, inc=1, device_id=at(far_peer(j), position), device_id_type=MESH
        )
    for j in range(1, NEAR):
        pl.semaphore_signal(barrier, inc=1, device_id=at(group, near_peer(j)), device_id_type=MESH)
    pl.semaphore_signal(barrier, inc=1, device_id={"det": 1 - det}, device_id_type=MESH)

    small = [
        pltpu.make_async_copy(dark_h, dark, small_sem.at[0]),
        pltpu.make_async_copy(exposure_h, exposure, small_sem.at[1]),
        pltpu.make_async_copy(aberration_h, aberration, small_sem.at[2]),
    ]
    loads = [pltpu.make_async_copy(row_tab, row_v, load_sem.at[0])]
    loads += [
        pltpu.make_async_copy(
            frames.at[:, :, pl.ds(c * LANES, LANES)], frames_v.at[c], load_sem.at[1 + c]
        )
        for c in range(chunks)
    ]
    loads.append(pltpu.make_async_copy(col_tab, col_v, load_sem.at[1 + chunks]))
    loads += [
        pltpu.make_async_copy(
            codes.at[:, :, pl.ds(c * LANES, LANES)], codes_v.at[c], load_sem.at[2 + chunks + c]
        )
        for c in range(chunks)
    ]
    first_loads = small + loads[: 1 + chunks]
    for load in first_loads:
        load.start()

    small[0].wait()
    near_buf[position] = jnp.sum(dark[...].astype(jnp.float32), axis=0, keepdims=True)
    loads[0].wait()
    m_tile = 512

    parts = []
    for c in range(chunks):
        count = rows // 2 if c in (0, chunks - 1) else rows
        parts += [(c, first, count) for first in range(0, rows, count)]

    def spectra(c):
        loads[1 + c].wait()
        for y in range(rows):
            joined[:, y * LANES : (y + 1) * LANES] = frames_v[c, y]
        for m in range(2 * nx // m_tile):
            part = jnp.dot(
                row_v[m * m_tile : (m + 1) * m_tile], joined[...],
                preferred_element_type=jnp.float32,
            )
            for y in range(rows):
                wide[pl.ds(m * m_tile * rows + y, m_tile, stride=rows), :] = part[
                    :, y * LANES : (y + 1) * LANES
                ]

        def narrow(g, carry):
            block = wide[pl.ds(pl.multiple_of(g * NEAR * q_rows, q_rows), NEAR * q_rows)]
            send[c, g] = block.astype(jnp.bfloat16).reshape(NEAR, q_rows, LANES)
            return carry

        lax.fori_loop(0, far, narrow, 0)
        recv[c, group, 0] = send[c, group, position]

    def ship_near(k):
        c, first, count = parts[k]
        span = pl.ds(first * unit, count * unit)
        for j in range(1, NEAR):
            peer = near_peer(j)
            pltpu.make_async_remote_copy(
                src_ref=send.at[c, :, peer, span], dst_ref=stage.at[c, :, NEAR - j, span],
                send_sem=near_send, recv_sem=near_recv.at[k],
                device_id=at(group, peer), device_id_type=MESH,
            ).start()

    def ship_own(k):
        c, first, count = parts[k]
        span = pl.ds(first * unit, count * unit)

        def one(j, carry):
            peer = far_peer(j)
            pltpu.make_async_remote_copy(
                src_ref=send.at[c, peer, position, span], dst_ref=recv.at[c, group, 0, span],
                send_sem=far_send, recv_sem=far_recv.at[k],
                device_id=at(peer, position), device_id_type=MESH,
            ).start()
            return carry

        lax.fori_loop(1, far, one, 0)

    def ship_far(k):
        c, first, count = parts[k]
        span = pl.ds(first * unit, count * unit)
        rest = pl.ds(1, NEAR - 1)

        def one(j, carry):
            peer = far_peer(j)
            pltpu.make_async_remote_copy(
                src_ref=stage.at[c, peer, rest, span], dst_ref=recv.at[c, group, rest, span],
                send_sem=far_send, recv_sem=far_recv.at[k],
                device_id=at(peer, position), device_id_type=MESH,
            ).start()
            return carry

        lax.fori_loop(1, far, one, 0)

    def arrive_near(k):
        c, first, count = parts[k]
        span = pl.ds(first * unit, count * unit)
        slots = stage.at[c, :, pl.ds(1, NEAR - 1), span]
        pltpu.make_async_copy(slots, slots, near_recv.at[k]).wait()
        recv[c, group, 1:, span] = stage[c, group, 1:, span]

    spectra(0)
    pl.semaphore_wait(barrier, NEAR + far - 1)

    ship_near(0)
    ship_own(0)
    ship_near(1)
    ship_own(1)
    for load in loads[1 + chunks :]:
        load.start()
    for j in range(1, NEAR):
        pltpu.make_async_remote_copy(
            src_ref=near_buf.at[position], dst_ref=near_buf.at[position],
            send_sem=dark_near_sem.at[0], recv_sem=dark_near_sem.at[1],
            device_id=at(group, near_peer(j)), device_id_type=MESH,
        ).start()
    for c in range(1, chunks):
        spectra(c)
        for k, part in enumerate(parts):
            if part[0] == c:
                ship_own(k)

    small[1].wait()
    turned = jnp.concatenate([exposure[...], jnp.zeros_like(exposure[...])], axis=0).T
    for y in range(rows):
        rest = jnp.broadcast_to(turned[:, y : y + 1], (nx, LANES))
        total = jnp.zeros((2 * nx, LANES), jnp.float32)
        for _ in range(3):
            high = rest.astype(jnp.bfloat16)
            total += jnp.dot(row_v[...], high, preferred_element_type=jnp.float32)
            rest = rest - high.astype(jnp.float32)
        wide[pl.ds(y, 2 * nx, stride=rows), :] = total
    per_row = LANES // q_rows
    per_group = NEAR // per_row
    diagonal = lax.broadcasted_iota(jnp.int32, (LANES, LANES), 0) == lax.broadcasted_iota(
        jnp.int32, (LANES, LANES), 1
    )

    def pack(g, carry):
        for h in range(per_group):
            start = pl.multiple_of((g * per_group + h) * LANES, LANES)
            row = jnp.where(diagonal, wide[pl.ds(start, LANES)], 0.0)
            level_out[h, pl.ds(g, 1)] = jnp.sum(row, axis=0, keepdims=True)
        return carry

    lax.fori_loop(0, far, pack, 0)
    half = lax.div(position, per_row)
    level_stage[0] = level_out[half]
    for j in range(1, NEAR):
        peer = near_peer(j)
        pltpu.make_async_remote_copy(
            src_ref=level_out.at[lax.div(peer, per_row)], dst_ref=level_stage.at[NEAR - j],
            send_sem=level_near_sem.at[0], recv_sem=level_near_sem.at[1],
            device_id=at(group, peer), device_id_type=MESH,
        ).start()
    for k in range(2, len(parts)):
        ship_near(k)

    arrive_near(0)
    ship_far(0)
    arrive_near(1)
    ship_far(1)

    near_some = near_buf.at[pl.ds(0, NEAR - 1)]
    pltpu.make_async_copy(near_some, near_some, dark_near_sem.at[1]).wait()
    far_buf[group] = jnp.sum(near_buf[...], axis=0)

    def send_dark(j, carry):
        pltpu.make_async_remote_copy(
            src_ref=far_buf.at[group], dst_ref=far_buf.at[group],
            send_sem=dark_far_sem.at[0], recv_sem=dark_far_sem.at[1],
            device_id=at(far_peer(j), position), device_id_type=MESH,
        ).start()
        return carry

    lax.fori_loop(1, far, send_dark, 0)


    level_near = level_stage.at[pl.ds(1, NEAR - 1)]
    pltpu.make_async_copy(level_near, level_near, level_near_sem.at[1]).wait()
    lane = lax.broadcasted_iota(jnp.int32, (far, LANES), 1)
    place = lax.rem(position, per_row)
    for h in range(per_group):
        row = jnp.zeros((far, LANES), jnp.float32)
        for m in range(per_row):
            block = jnp.where(lane // q_rows == place, level_stage[h * per_row + m], 0.0)
            row += pltpu.roll(block, lax.rem((m - place + per_row) * q_rows, LANES), axis=1)
        level_pack[h] = row.reshape(far, 1, LANES)
    level_in[:, group] = level_pack[:, group]

    def send_level(j, carry):
        peer = far_peer(j)
        pltpu.make_async_remote_copy(
            src_ref=level_pack.at[:, peer], dst_ref=level_in.at[:, group],
            send_sem=level_far_sem.at[0], recv_sem=level_far_sem.at[1],
            device_id=at(peer, position), device_id_type=MESH,
        ).start()
        return carry

    lax.fori_loop(1, far, send_level, 0)

    for k in range(2, len(parts)):
        arrive_near(k)
        ship_far(k)

    small[2].wait()
    angle = jnp.broadcast_to(aberration[...], (8, aberration.shape[1]))
    cos, sin = jnp.cos(angle), jnp.sin(angle)
    for c in range(chunks):
        turn[c, 0] = cos[:, c * LANES : (c + 1) * LANES]
        turn[c, 1] = sin[:, c * LANES : (c + 1) * LANES]
    acc[...] = jnp.zeros_like(acc)
    level_far = level_in.at[:, pl.ds(0, far - 1)]
    pltpu.make_async_copy(level_far, level_far, level_far_sem.at[1]).wait()
    columns = level_in[...].reshape(per_group * far, LANES).T
    index = lax.broadcasted_iota(jnp.int32, (q_rows, per_group * far), 1)

    def unpack(g, carry):
        for h in range(per_group):
            for m in range(per_row):
                block = jnp.where(index == h * far + g, columns[m * q_rows : (m + 1) * q_rows], 0.0)
                level[g, h * per_row + m] = jnp.broadcast_to(
                    jnp.sum(block, axis=1, keepdims=True), (q_rows, LANES)
                )
        return carry

    lax.fori_loop(0, far, unpack, 0)
    far_some = far_buf.at[pl.ds(0, far - 1)]
    pltpu.make_async_copy(far_some, far_some, dark_far_sem.at[1]).wait()
    mean = jnp.sum(far_buf[...], axis=0) / frame_total
    for c in range(chunks):
        dark_row[c] = jnp.broadcast_to(mean[:, c * LANES : (c + 1) * LANES], (8, LANES))

    loads[1 + chunks].wait()

    def weigh(k):
        c, first, count = parts[k]
        if first == 0:
            loads[2 + chunks + c].wait()
        span = pl.ds(first * unit, count * unit)
        others = recv.at[c, pl.ds(0, far - 1), :, span]
        pltpu.make_async_copy(others, others, far_recv.at[k]).wait()
        dark_mean = jnp.broadcast_to(dark_row[c, 0:1], (count * unit, LANES))

        def regroup(g, carry):
            for m in range(NEAR // 2):
                blocks = []
                for source in (2 * m, 2 * m + 1):
                    slot = lax.rem(source - position + NEAR, NEAR)
                    block = recv[c, g, slot, span].astype(jnp.float32)
                    blocks.append(block - level[g, slot, span] * dark_mean)
                to = pl.ds(pl.multiple_of((g * NEAR + 2 * m) * unit, 2 * unit), 2 * unit)
                for q in range(count):
                    pair = [block[q * unit : (q + 1) * unit] for block in blocks]
                    gathered[to, q * LANES : (q + 1) * LANES] = jnp.concatenate(
                        pair, axis=0
                    ).astype(jnp.bfloat16)
            return carry

        lax.fori_loop(0, far, regroup, 0)
        cos = jnp.broadcast_to(turn[c, 0, 0:1], (tile, LANES))
        sin = jnp.broadcast_to(turn[c, 1, 0:1], (tile, LANES))

        def column(t, carry):
            full = jnp.dot(
                col_v[t], gathered[:, : count * LANES], preferred_element_type=jnp.float32
            )
            here = pl.ds(pl.multiple_of(t * tile, tile), tile)
            for q in range(count):
                real = full[:tile, q * LANES : (q + 1) * LANES]
                imag = full[tile:, q * LANES : (q + 1) * LANES]
                code = codes_v[c, first + q, here]
                weight = (code == 1).astype(jnp.float32) - (code == 2).astype(jnp.float32)
                acc[first + q, here] += weight * (real * cos + imag * sin)
                acc[rows + first + q, here] += weight * (imag * cos - real * sin)
            return carry

        lax.fori_loop(0, col_v.shape[0], column, 0)

    for k in range(len(parts)):
        weigh(k)

    row = lax.broadcasted_iota(jnp.int32, (2 * rows, LANES), 0)
    total = jnp.zeros((2 * rows, acc.shape[1]), jnp.float32)
    for i in range(2 * rows):
        pick = (row == i).astype(jnp.bfloat16)
        value = acc[i]
        for _ in range(2):
            high = value.astype(jnp.bfloat16)
            total += lax.dot_general(
                pick, high, (((1,), (1,)), ((), ())), preferred_element_type=jnp.float32
            )
            value = value - high.astype(jnp.float32)
    total = total / scale
    width = half_in.shape[1]
    halves[0] = total[:, :width]
    halves[1] = total[:, width:]
    swap = pltpu.make_async_remote_copy(
        src_ref=halves.at[1 - det], dst_ref=half_in, send_sem=det_sem.at[0],
        recv_sem=det_sem.at[1], device_id={"det": 1 - det}, device_id_type=MESH,
    )
    swap.start()

    pltpu.make_async_copy(near_some, near_some, dark_near_sem.at[0]).wait()
    pltpu.make_async_copy(far_some, far_some, dark_far_sem.at[0]).wait()
    pltpu.make_async_copy(level_near, level_near, level_near_sem.at[0]).wait()
    pltpu.make_async_copy(level_far, level_far, level_far_sem.at[0]).wait()
    slots = stage.at[:, :, pl.ds(1, NEAR - 1)]
    pltpu.make_async_copy(slots, slots, near_send).wait()
    others = recv.at[:, pl.ds(0, far - 1)]
    pltpu.make_async_copy(others, others, far_send).wait()

    swap.wait()
    result = halves[det] + half_in[...]
    out[0] = result[:rows]
    out[1] = result[rows:]


def solution(mesh):
    n = mesh.shape["scan"]

    def on_device(frames, exposure, dark_counts, aberration, margin_codes):
        rows, nx, pix = frames.shape
        ny = rows * n
        chunks = pix // LANES
        tile = 256
        far = n // NEAR
        q_rows = 2 * rows * rows
        row_tab = row_table(nx)
        col_tab = column_table(ny, rows, tile)
        hbm = pl.BlockSpec(memory_space=pl.ANY)
        vmem = pl.BlockSpec(memory_space=pltpu.VMEM)
        body = functools.partial(
            kernel, n, rows, chunks, tile, dark_counts.shape[0] * n,
            math.sqrt(pix * mesh.shape["det"]),
        )
        spectra = pltpu.VMEM((chunks, far, NEAR, q_rows, LANES), jnp.bfloat16)
        packed = pltpu.VMEM((NEAR * q_rows // LANES, far, 1, LANES), jnp.float32)
        return pl.pallas_call(
            body,
            out_shape=jax.ShapeDtypeStruct((2, rows, ny // mesh.shape["det"]), jnp.float32),
            in_specs=[hbm] * 7,
            out_specs=vmem,
            scratch_shapes=[
                pltpu.VMEM((rows, nx), jnp.float32),
                pltpu.VMEM(dark_counts.shape, jnp.int32),
                pltpu.VMEM((1, pix), jnp.float32),
                pltpu.VMEM((chunks, rows, nx, LANES), jnp.bfloat16),
                pltpu.VMEM((chunks, rows, ny, LANES), jnp.int32),
                pltpu.VMEM(row_tab.shape, jnp.bfloat16),
                pltpu.VMEM(col_tab.shape, jnp.bfloat16),
                pltpu.VMEM((nx, rows * LANES), jnp.bfloat16),
                pltpu.VMEM((n * q_rows, LANES), jnp.float32),
                pltpu.VMEM((far, NEAR, q_rows, LANES), jnp.float32),
                spectra,
                spectra,
                spectra,
                pltpu.VMEM((2 * ny, rows * LANES), jnp.bfloat16),
                pltpu.VMEM((2 * rows, ny, LANES), jnp.float32),
                pltpu.VMEM((NEAR, 1, pix), jnp.float32),
                pltpu.VMEM((far, 1, pix), jnp.float32),
                pltpu.VMEM((chunks, 8, LANES), jnp.float32),
                pltpu.VMEM((chunks, 2, 8, LANES), jnp.float32),
                pltpu.VMEM((NEAR * q_rows // LANES, far, LANES), jnp.float32),
                pltpu.VMEM((NEAR, far, LANES), jnp.float32),
                packed,
                packed,
                pltpu.VMEM((2, 2 * rows, ny // 2), jnp.float32),
                pltpu.VMEM((2 * rows, ny // 2), jnp.float32),
                pltpu.SemaphoreType.DMA((3,)),
                pltpu.SemaphoreType.DMA((2 + 2 * chunks,)),
                pltpu.SemaphoreType.DMA((2,)),
                pltpu.SemaphoreType.DMA((2,)),
                pltpu.SemaphoreType.DMA((2,)),
                pltpu.SemaphoreType.DMA((2,)),
                pltpu.SemaphoreType.DMA,
                pltpu.SemaphoreType.DMA((chunks + 2,)),
                pltpu.SemaphoreType.DMA,
                pltpu.SemaphoreType.DMA((chunks + 2,)),
                pltpu.SemaphoreType.DMA((2,)),
            ],
            compiler_params=pltpu.CompilerParams(
                collective_id=0, has_side_effects=True, vmem_limit_bytes=63 * 1024 * 1024
            ),
        )(
            frames, exposure, dark_counts, aberration.reshape(1, pix), margin_codes,
            jnp.asarray(row_tab), jnp.asarray(col_tab),
        )

    placed = (
        P("scan", None, "det"),
        P("scan", None),
        P("scan", "det"),
        P("det"),
        P("scan", None, "det"),
    )
    return jax.shard_map(
        on_device, mesh=mesh, in_specs=placed, out_specs=P(None, "scan", "det"), check_vma=False
    )
```

```python
import functools
import math

import jax
import jax.numpy as jnp
import ml_dtypes
import numpy as np
from jax import lax
from jax.experimental import pallas as pl
from jax.experimental.pallas import tpu as pltpu
from jax.sharding import PartitionSpec as P

MESH = pl.DeviceIdType.MESH
LANES = 128
NEAR = 8


def dft_tables(length):
    index_row = np.arange(length, dtype=np.int64)
    products = (index_row[:, None] * index_row[None, :] % length).astype(np.float32)
    phase = np.float32(2.0 * math.pi / length) * products
    scale = np.float32(1.0 / math.sqrt(length))
    return (
        (np.cos(phase) * scale).astype(ml_dtypes.bfloat16),
        (-np.sin(phase) * scale).astype(ml_dtypes.bfloat16),
    )


def row_table(length):
    cos, sin = dft_tables(length)
    return np.stack([cos.T, sin.T], axis=1).reshape(2 * length, length)


def column_table(length, rows, tile):
    cos, sin = dft_tables(length)
    real = np.stack([cos, -sin], axis=1)
    imag = np.stack([sin, cos], axis=1)
    both = np.stack([real, imag]).reshape(2, length, 2, length // rows, rows)
    both = both.transpose(0, 1, 3, 2, 4).reshape(2, length // tile, tile, 2 * length)
    return np.ascontiguousarray(both.transpose(1, 0, 2, 3)).reshape(
        length // tile, 2 * tile, 2 * length
    )


def kernel(
    n, rows, chunks, tile, frame_total, scale,
    frames, exposure_h, dark_h, aberration_h, codes, row_tab, col_tab, out,
    exposure, dark, aberration,
    frames_v, codes_v, row_v, col_v, joined, wide, level, send, stage, recv, gathered, acc,
    near_buf, far_buf, dark_row, turn, level_out, level_stage, level_pack, level_in, halves, half_in,
    small_sem, load_sem, dark_near_sem, dark_far_sem, level_near_sem, level_far_sem,
    near_send, near_recv, far_send, far_recv, det_sem,
):
    me = lax.axis_index("scan")
    det = lax.axis_index("det")
    nx = frames_v.shape[2]
    unit = 2 * rows
    q_rows = unit * rows
    far = n // NEAR
    position = lax.rem(me, NEAR)
    group = lax.div(me, NEAR)

    def near_peer(j):
        return lax.rem(position + j, NEAR)

    cross = (group >> 2) & 1

    def far_peer(j):
        step = jnp.int32(j) - 1
        first = step < 7 + cross
        high = jnp.where(first, cross, 1 - cross)
        base = jnp.where(first, step + 1 - cross, step - 7)
        return group ^ ((base & 3) | ((base & 4) << 1) | (high << 2))

    def at(g, p):
        return {"scan": g * NEAR + p}

    barrier = pltpu.get_barrier_semaphore()
    for j in range(1, far):
        pl.semaphore_signal(
            barrier, inc=1, device_id=at(far_peer(j), position), device_id_type=MESH
        )
    for j in range(1, NEAR):
        pl.semaphore_signal(barrier, inc=1, device_id=at(group, near_peer(j)), device_id_type=MESH)
    pl.semaphore_signal(barrier, inc=1, device_id={"det": 1 - det}, device_id_type=MESH)

    small = [
        pltpu.make_async_copy(dark_h, dark, small_sem.at[0]),
        pltpu.make_async_copy(exposure_h, exposure, small_sem.at[1]),
        pltpu.make_async_copy(aberration_h, aberration, small_sem.at[2]),
    ]
    loads = [pltpu.make_async_copy(row_tab, row_v, load_sem.at[0])]
    loads += [
        pltpu.make_async_copy(
            frames.at[:, :, pl.ds(c * LANES, LANES)], frames_v.at[c], load_sem.at[1 + c]
        )
        for c in range(chunks)
    ]
    loads.append(pltpu.make_async_copy(col_tab, col_v, load_sem.at[1 + chunks]))
    loads += [
        pltpu.make_async_copy(
            codes.at[:, :, pl.ds(c * LANES, LANES)], codes_v.at[c], load_sem.at[2 + chunks + c]
        )
        for c in range(chunks)
    ]
    first_loads = small + loads[: 1 + chunks]
    for load in first_loads:
        load.start()

    small[0].wait()
    near_buf[position] = jnp.sum(dark[...].astype(jnp.float32), axis=0, keepdims=True)
    loads[0].wait()
    m_tile = 512

    parts = []
    for c in range(chunks):
        count = rows // 2 if c in (0, chunks - 1) else rows
        parts += [(c, first, count) for first in range(0, rows, count)]

    def spectra(c):
        loads[1 + c].wait()
        for y in range(rows):
            joined[:, y * LANES : (y + 1) * LANES] = frames_v[c, y]
        for m in range(2 * nx // m_tile):
            part = jnp.dot(
                row_v[m * m_tile : (m + 1) * m_tile], joined[...],
                preferred_element_type=jnp.float32,
            )
            for y in range(rows):
                wide[pl.ds(m * m_tile * rows + y, m_tile, stride=rows), :] = part[
                    :, y * LANES : (y + 1) * LANES
                ]

        def narrow(g, carry):
            block = wide[pl.ds(pl.multiple_of(g * NEAR * q_rows, q_rows), NEAR * q_rows)]
            send[c, g] = block.astype(jnp.bfloat16).reshape(NEAR, q_rows, LANES)
            return carry

        lax.fori_loop(0, far, narrow, 0)
        recv[c, group, 0] = send[c, group, position]

    def ship_near(k):
        c, first, count = parts[k]
        span = pl.ds(first * unit, count * unit)
        for j in range(1, NEAR):
            peer = near_peer(j)
            pltpu.make_async_remote_copy(
                src_ref=send.at[c, :, peer, span], dst_ref=stage.at[c, :, NEAR - j, span],
                send_sem=near_send, recv_sem=near_recv.at[k],
                device_id=at(group, peer), device_id_type=MESH,
            ).start()

    def ship_own(k):
        c, first, count = parts[k]
        span = pl.ds(first * unit, count * unit)

        def one(j, carry):
            peer = far_peer(j)
            pltpu.make_async_remote_copy(
                src_ref=send.at[c, peer, position, span], dst_ref=recv.at[c, group, 0, span],
                send_sem=far_send, recv_sem=far_recv.at[k],
                device_id=at(peer, position), device_id_type=MESH,
            ).start()
            return carry

        lax.fori_loop(1, far, one, 0)

    def ship_far(k):
        c, first, count = parts[k]
        span = pl.ds(first * unit, count * unit)
        rest = pl.ds(1, NEAR - 1)

        def one(j, carry):
            peer = far_peer(j)
            pltpu.make_async_remote_copy(
                src_ref=stage.at[c, peer, rest, span], dst_ref=recv.at[c, group, rest, span],
                send_sem=far_send, recv_sem=far_recv.at[k],
                device_id=at(peer, position), device_id_type=MESH,
            ).start()
            return carry

        lax.fori_loop(1, far, one, 0)

    def arrive_near(k):
        c, first, count = parts[k]
        span = pl.ds(first * unit, count * unit)
        slots = stage.at[c, :, pl.ds(1, NEAR - 1), span]
        pltpu.make_async_copy(slots, slots, near_recv.at[k]).wait()
        recv[c, group, 1:, span] = stage[c, group, 1:, span]

    spectra(0)
    pl.semaphore_wait(barrier, NEAR + far - 1)

    ship_near(0)
    ship_own(0)
    ship_near(1)
    ship_own(1)
    for load in loads[1 + chunks :]:
        load.start()
    for j in range(1, NEAR):
        pltpu.make_async_remote_copy(
            src_ref=near_buf.at[position], dst_ref=near_buf.at[position],
            send_sem=dark_near_sem.at[0], recv_sem=dark_near_sem.at[1],
            device_id=at(group, near_peer(j)), device_id_type=MESH,
        ).start()
    for c in range(1, chunks):
        spectra(c)
        for k, part in enumerate(parts):
            if part[0] == c:
                ship_own(k)

    small[1].wait()
    turned = jnp.concatenate([exposure[...], jnp.zeros_like(exposure[...])], axis=0).T
    for y in range(rows):
        rest = jnp.broadcast_to(turned[:, y : y + 1], (nx, LANES))
        total = jnp.zeros((2 * nx, LANES), jnp.float32)
        for _ in range(3):
            high = rest.astype(jnp.bfloat16)
            total += jnp.dot(row_v[...], high, preferred_element_type=jnp.float32)
            rest = rest - high.astype(jnp.float32)
        wide[pl.ds(y, 2 * nx, stride=rows), :] = total
    per_row = LANES // q_rows
    per_group = NEAR // per_row
    diagonal = lax.broadcasted_iota(jnp.int32, (LANES, LANES), 0) == lax.broadcasted_iota(
        jnp.int32, (LANES, LANES), 1
    )

    def pack(g, carry):
        for h in range(per_group):
            start = pl.multiple_of((g * per_group + h) * LANES, LANES)
            row = jnp.where(diagonal, wide[pl.ds(start, LANES)], 0.0)
            level_out[h, pl.ds(g, 1)] = jnp.sum(row, axis=0, keepdims=True)
        return carry

    lax.fori_loop(0, far, pack, 0)
    half = lax.div(position, per_row)
    level_stage[0] = level_out[half]
    for j in range(1, NEAR):
        peer = near_peer(j)
        pltpu.make_async_remote_copy(
            src_ref=level_out.at[lax.div(peer, per_row)], dst_ref=level_stage.at[NEAR - j],
            send_sem=level_near_sem.at[0], recv_sem=level_near_sem.at[1],
            device_id=at(group, peer), device_id_type=MESH,
        ).start()
    for k in range(2, len(parts)):
        ship_near(k)

    arrive_near(0)
    ship_far(0)
    arrive_near(1)
    ship_far(1)

    near_some = near_buf.at[pl.ds(0, NEAR - 1)]
    pltpu.make_async_copy(near_some, near_some, dark_near_sem.at[1]).wait()
    far_buf[group] = jnp.sum(near_buf[...], axis=0)

    def send_dark(j, carry):
        pltpu.make_async_remote_copy(
            src_ref=far_buf.at[group], dst_ref=far_buf.at[group],
            send_sem=dark_far_sem.at[0], recv_sem=dark_far_sem.at[1],
            device_id=at(far_peer(j), position), device_id_type=MESH,
        ).start()
        return carry

    lax.fori_loop(1, far, send_dark, 0)


    level_near = level_stage.at[pl.ds(1, NEAR - 1)]
    pltpu.make_async_copy(level_near, level_near, level_near_sem.at[1]).wait()
    lane = lax.broadcasted_iota(jnp.int32, (far, LANES), 1)
    place = lax.rem(position, per_row)
    for h in range(per_group):
        row = jnp.zeros((far, LANES), jnp.float32)
        for m in range(per_row):
            block = jnp.where(lane // q_rows == place, level_stage[h * per_row + m], 0.0)
            row += pltpu.roll(block, lax.rem((m - place + per_row) * q_rows, LANES), axis=1)
        level_pack[h] = row.reshape(far, 1, LANES)
    level_in[:, group] = level_pack[:, group]

    def send_level(j, carry):
        peer = far_peer(j)
        pltpu.make_async_remote_copy(
            src_ref=level_pack.at[:, peer], dst_ref=level_in.at[:, group],
            send_sem=level_far_sem.at[0], recv_sem=level_far_sem.at[1],
            device_id=at(peer, position), device_id_type=MESH,
        ).start()
        return carry

    lax.fori_loop(1, far, send_level, 0)

    for k in range(2, len(parts)):
        arrive_near(k)
        ship_far(k)

    small[2].wait()
    angle = jnp.broadcast_to(aberration[...], (8, aberration.shape[1]))
    cos, sin = jnp.cos(angle), jnp.sin(angle)
    for c in range(chunks):
        turn[c, 0] = cos[:, c * LANES : (c + 1) * LANES]
        turn[c, 1] = sin[:, c * LANES : (c + 1) * LANES]
    acc[...] = jnp.zeros_like(acc)
    level_far = level_in.at[:, pl.ds(0, far - 1)]
    pltpu.make_async_copy(level_far, level_far, level_far_sem.at[1]).wait()
    columns = level_in[...].reshape(per_group * far, LANES).T
    index = lax.broadcasted_iota(jnp.int32, (q_rows, per_group * far), 1)

    def unpack(g, carry):
        for h in range(per_group):
            for m in range(per_row):
                block = jnp.where(index == h * far + g, columns[m * q_rows : (m + 1) * q_rows], 0.0)
                level[g, h * per_row + m] = jnp.broadcast_to(
                    jnp.sum(block, axis=1, keepdims=True), (q_rows, LANES)
                )
        return carry

    lax.fori_loop(0, far, unpack, 0)
    far_some = far_buf.at[pl.ds(0, far - 1)]
    pltpu.make_async_copy(far_some, far_some, dark_far_sem.at[1]).wait()
    mean = jnp.sum(far_buf[...], axis=0) / frame_total
    for c in range(chunks):
        dark_row[c] = jnp.broadcast_to(mean[:, c * LANES : (c + 1) * LANES], (8, LANES))

    loads[1 + chunks].wait()

    def weigh(k):
        c, first, count = parts[k]
        if first == 0:
            loads[2 + chunks + c].wait()
        span = pl.ds(first * unit, count * unit)
        others = recv.at[c, pl.ds(0, far - 1), :, span]
        pltpu.make_async_copy(others, others, far_recv.at[k]).wait()
        dark_mean = jnp.broadcast_to(dark_row[c, 0:1], (count * unit, LANES))

        def regroup(g, carry):
            for m in range(NEAR // 2):
                blocks = []
                for source in (2 * m, 2 * m + 1):
                    slot = lax.rem(source - position + NEAR, NEAR)
                    block = recv[c, g, slot, span].astype(jnp.float32)
                    blocks.append(block - level[g, slot, span] * dark_mean)
                to = pl.ds(pl.multiple_of((g * NEAR + 2 * m) * unit, 2 * unit), 2 * unit)
                for q in range(count):
                    pair = [block[q * unit : (q + 1) * unit] for block in blocks]
                    gathered[to, q * LANES : (q + 1) * LANES] = jnp.concatenate(
                        pair, axis=0
                    ).astype(jnp.bfloat16)
            return carry

        lax.fori_loop(0, far, regroup, 0)
        cos = jnp.broadcast_to(turn[c, 0, 0:1], (tile, LANES))
        sin = jnp.broadcast_to(turn[c, 1, 0:1], (tile, LANES))

        def column(t, carry):
            full = jnp.dot(
                col_v[t], gathered[:, : count * LANES], preferred_element_type=jnp.float32
            )
            here = pl.ds(pl.multiple_of(t * tile, tile), tile)
            for q in range(count):
                real = full[:tile, q * LANES : (q + 1) * LANES]
                imag = full[tile:, q * LANES : (q + 1) * LANES]
                code = codes_v[c, first + q, here]
                weight = (code == 1).astype(jnp.float32) - (code == 2).astype(jnp.float32)
                acc[first + q, here] += weight * (real * cos + imag * sin)
                acc[rows + first + q, here] += weight * (imag * cos - real * sin)
            return carry

        lax.fori_loop(0, col_v.shape[0], column, 0)

    for k in range(len(parts)):
        weigh(k)

    row = lax.broadcasted_iota(jnp.int32, (2 * rows, LANES), 0)
    total = jnp.zeros((2 * rows, acc.shape[1]), jnp.float32)
    for i in range(2 * rows):
        pick = (row == i).astype(jnp.bfloat16)
        value = acc[i]
        for _ in range(2):
            high = value.astype(jnp.bfloat16)
            total += lax.dot_general(
                pick, high, (((1,), (1,)), ((), ())), preferred_element_type=jnp.float32
            )
            value = value - high.astype(jnp.float32)
    total = total / scale
    width = half_in.shape[1]
    halves[0] = total[:, :width]
    halves[1] = total[:, width:]
    swap = pltpu.make_async_remote_copy(
        src_ref=halves.at[1 - det], dst_ref=half_in, send_sem=det_sem.at[0],
        recv_sem=det_sem.at[1], device_id={"det": 1 - det}, device_id_type=MESH,
    )
    swap.start()

    pltpu.make_async_copy(near_some, near_some, dark_near_sem.at[0]).wait()
    pltpu.make_async_copy(far_some, far_some, dark_far_sem.at[0]).wait()
    pltpu.make_async_copy(level_near, level_near, level_near_sem.at[0]).wait()
    pltpu.make_async_copy(level_far, level_far, level_far_sem.at[0]).wait()
    slots = stage.at[:, :, pl.ds(1, NEAR - 1)]
    pltpu.make_async_copy(slots, slots, near_send).wait()
    others = recv.at[:, pl.ds(0, far - 1)]
    pltpu.make_async_copy(others, others, far_send).wait()

    swap.wait()
    result = halves[det] + half_in[...]
    out[0] = result[:rows]
    out[1] = result[rows:]


def solution(mesh):
    n = mesh.shape["scan"]

    def on_device(frames, exposure, dark_counts, aberration, margin_codes):
        rows, nx, pix = frames.shape
        ny = rows * n
        chunks = pix // LANES
        tile = 256
        far = n // NEAR
        q_rows = 2 * rows * rows
        row_tab = row_table(nx)
        col_tab = column_table(ny, rows, tile)
        hbm = pl.BlockSpec(memory_space=pl.ANY)
        vmem = pl.BlockSpec(memory_space=pltpu.VMEM)
        body = functools.partial(
            kernel, n, rows, chunks, tile, dark_counts.shape[0] * n,
            math.sqrt(pix * mesh.shape["det"]),
        )
        spectra = pltpu.VMEM((chunks, far, NEAR, q_rows, LANES), jnp.bfloat16)
        packed = pltpu.VMEM((NEAR * q_rows // LANES, far, 1, LANES), jnp.float32)
        return pl.pallas_call(
            body,
            out_shape=jax.ShapeDtypeStruct((2, rows, ny // mesh.shape["det"]), jnp.float32),
            in_specs=[hbm] * 7,
            out_specs=vmem,
            scratch_shapes=[
                pltpu.VMEM((rows, nx), jnp.float32),
                pltpu.VMEM(dark_counts.shape, jnp.int32),
                pltpu.VMEM((1, pix), jnp.float32),
                pltpu.VMEM((chunks, rows, nx, LANES), jnp.bfloat16),
                pltpu.VMEM((chunks, rows, ny, LANES), jnp.int32),
                pltpu.VMEM(row_tab.shape, jnp.bfloat16),
                pltpu.VMEM(col_tab.shape, jnp.bfloat16),
                pltpu.VMEM((nx, rows * LANES), jnp.bfloat16),
                pltpu.VMEM((n * q_rows, LANES), jnp.float32),
                pltpu.VMEM((far, NEAR, q_rows, LANES), jnp.float32),
                spectra,
                spectra,
                spectra,
                pltpu.VMEM((2 * ny, rows * LANES), jnp.bfloat16),
                pltpu.VMEM((2 * rows, ny, LANES), jnp.float32),
                pltpu.VMEM((NEAR, 1, pix), jnp.float32),
                pltpu.VMEM((far, 1, pix), jnp.float32),
                pltpu.VMEM((chunks, 8, LANES), jnp.float32),
                pltpu.VMEM((chunks, 2, 8, LANES), jnp.float32),
                pltpu.VMEM((NEAR * q_rows // LANES, far, LANES), jnp.float32),
                pltpu.VMEM((NEAR, far, LANES), jnp.float32),
                packed,
                packed,
                pltpu.VMEM((2, 2 * rows, ny // 2), jnp.float32),
                pltpu.VMEM((2 * rows, ny // 2), jnp.float32),
                pltpu.SemaphoreType.DMA((3,)),
                pltpu.SemaphoreType.DMA((2 + 2 * chunks,)),
                pltpu.SemaphoreType.DMA((2,)),
                pltpu.SemaphoreType.DMA((2,)),
                pltpu.SemaphoreType.DMA((2,)),
                pltpu.SemaphoreType.DMA((2,)),
                pltpu.SemaphoreType.DMA,
                pltpu.SemaphoreType.DMA((chunks + 2,)),
                pltpu.SemaphoreType.DMA,
                pltpu.SemaphoreType.DMA((chunks + 2,)),
                pltpu.SemaphoreType.DMA((2,)),
            ],
            compiler_params=pltpu.CompilerParams(
                collective_id=0, has_side_effects=True, vmem_limit_bytes=63 * 1024 * 1024
            ),
        )(
            frames, exposure, dark_counts, aberration.reshape(1, pix), margin_codes,
            jnp.asarray(row_tab), jnp.asarray(col_tab),
        )

    placed = (
        P("scan", None, "det"),
        P("scan", None),
        P("scan", "det"),
        P("det"),
        P("scan", None, "det"),
    )
    return jax.shard_map(
        on_device, mesh=mesh, in_specs=placed, out_specs=P(None, "scan", "det"), check_vma=False
    )
```

```python
import functools
import math

import jax
import jax.numpy as jnp
import ml_dtypes
import numpy as np
from jax import lax
from jax.experimental import pallas as pl
from jax.experimental.pallas import tpu as pltpu
from jax.sharding import PartitionSpec as P

MESH = pl.DeviceIdType.MESH
LANES = 128
NEAR = 8


def dft_tables(length):
    index_row = np.arange(length, dtype=np.int64)
    products = (index_row[:, None] * index_row[None, :] % length).astype(np.float32)
    phase = np.float32(2.0 * math.pi / length) * products
    scale = np.float32(1.0 / math.sqrt(length))
    return (
        (np.cos(phase) * scale).astype(ml_dtypes.bfloat16),
        (-np.sin(phase) * scale).astype(ml_dtypes.bfloat16),
    )


def row_table(length):
    cos, sin = dft_tables(length)
    return np.stack([cos.T, sin.T], axis=1).reshape(2 * length, length)


def column_table(length, rows, tile):
    cos, sin = dft_tables(length)
    real = np.stack([cos, -sin], axis=1)
    imag = np.stack([sin, cos], axis=1)
    both = np.stack([real, imag]).reshape(2, length, 2, length // rows, rows)
    both = both.transpose(0, 1, 3, 2, 4).reshape(2, length // tile, tile, 2 * length)
    return np.ascontiguousarray(both.transpose(1, 0, 2, 3)).reshape(
        length // tile, 2 * tile, 2 * length
    )


def kernel(
    n, rows, chunks, tile, frame_total, scale,
    frames, exposure_h, dark_h, aberration_h, codes, row_tab, col_tab, out,
    exposure, dark, aberration,
    frames_v, codes_v, row_v, col_v, joined, wide, level, send, stage, recv, gathered, acc,
    near_buf, far_buf, dark_row, turn, level_out, level_stage, level_pack, level_in, halves, half_in,
    small_sem, load_sem, dark_near_sem, dark_far_sem, dark_row_sem, level_near_sem, level_far_sem,
    near_send, near_recv, far_send, far_recv, det_sem,
):
    me = lax.axis_index("scan")
    det = lax.axis_index("det")
    nx = frames_v.shape[2]
    unit = 2 * rows
    q_rows = unit * rows
    far = n // NEAR
    position = lax.rem(me, NEAR)
    group = lax.div(me, NEAR)

    def near_peer(j):
        return lax.rem(position + j, NEAR)

    cross = (group >> 2) & 1

    def far_peer(j):
        step = jnp.int32(j) - 1
        first = step < 7 + cross
        high = jnp.where(first, cross, 1 - cross)
        base = jnp.where(first, step + 1 - cross, step - 7)
        return group ^ ((base & 3) | ((base & 4) << 1) | (high << 2))

    def at(g, p):
        return {"scan": g * NEAR + p}

    barrier = pltpu.get_barrier_semaphore()
    for j in range(1, far):
        pl.semaphore_signal(
            barrier, inc=1, device_id=at(far_peer(j), position), device_id_type=MESH
        )
    for j in range(1, NEAR):
        pl.semaphore_signal(barrier, inc=1, device_id=at(group, near_peer(j)), device_id_type=MESH)
    pl.semaphore_signal(barrier, inc=1, device_id={"det": 1 - det}, device_id_type=MESH)

    small = [
        pltpu.make_async_copy(dark_h, dark, small_sem.at[0]),
        pltpu.make_async_copy(exposure_h, exposure, small_sem.at[1]),
        pltpu.make_async_copy(aberration_h, aberration, small_sem.at[2]),
    ]
    loads = [pltpu.make_async_copy(row_tab, row_v, load_sem.at[0])]
    loads += [
        pltpu.make_async_copy(
            frames.at[:, :, pl.ds(c * LANES, LANES)], frames_v.at[c], load_sem.at[1 + c]
        )
        for c in range(chunks)
    ]
    loads.append(pltpu.make_async_copy(col_tab, col_v, load_sem.at[1 + chunks]))
    loads += [
        pltpu.make_async_copy(
            codes.at[:, :, pl.ds(c * LANES, LANES)], codes_v.at[c], load_sem.at[2 + chunks + c]
        )
        for c in range(chunks)
    ]
    first_loads = small + loads[: 1 + chunks]
    for load in first_loads:
        load.start()

    small[0].wait()
    counted = jnp.sum(dark[...].astype(jnp.float32), axis=0, keepdims=True)
    for c in range(chunks):
        near_buf[c, position] = counted[:, c * LANES : (c + 1) * LANES]
    loads[0].wait()
    m_tile = 512

    parts = []
    for c in range(chunks):
        count = rows // 2 if c in (0, chunks - 1) else rows
        parts += [(c, first, count) for first in range(0, rows, count)]

    def spectra(c):
        loads[1 + c].wait()
        for y in range(rows):
            joined[:, y * LANES : (y + 1) * LANES] = frames_v[c, y]
        for m in range(2 * nx // m_tile):
            part = jnp.dot(
                row_v[m * m_tile : (m + 1) * m_tile], joined[...],
                preferred_element_type=jnp.float32,
            )
            for y in range(rows):
                wide[pl.ds(m * m_tile * rows + y, m_tile, stride=rows), :] = part[
                    :, y * LANES : (y + 1) * LANES
                ]

        def narrow(g, carry):
            block = wide[pl.ds(pl.multiple_of(g * NEAR * q_rows, q_rows), NEAR * q_rows)]
            send[c, g] = block.astype(jnp.bfloat16).reshape(NEAR, q_rows, LANES)
            return carry

        lax.fori_loop(0, far, narrow, 0)
        recv[c, group, 0] = send[c, group, position]

    def ship_near(k):
        c, first, count = parts[k]
        span = pl.ds(first * unit, count * unit)
        for j in range(1, NEAR):
            peer = near_peer(j)
            pltpu.make_async_remote_copy(
                src_ref=send.at[c, :, peer, span], dst_ref=stage.at[c, :, NEAR - j, span],
                send_sem=near_send, recv_sem=near_recv.at[k],
                device_id=at(group, peer), device_id_type=MESH,
            ).start()

    def ship_own(k):
        c, first, count = parts[k]
        span = pl.ds(first * unit, count * unit)

        def one(j, carry):
            peer = far_peer(j)
            pltpu.make_async_remote_copy(
                src_ref=send.at[c, peer, position, span], dst_ref=recv.at[c, group, 0, span],
                send_sem=far_send, recv_sem=far_recv.at[k],
                device_id=at(peer, position), device_id_type=MESH,
            ).start()
            return carry

        lax.fori_loop(1, far, one, 0)

    def ship_far(k):
        c, first, count = parts[k]
        span = pl.ds(first * unit, count * unit)
        rest = pl.ds(1, NEAR - 1)

        def one(j, carry):
            peer = far_peer(j)
            pltpu.make_async_remote_copy(
                src_ref=stage.at[c, peer, rest, span], dst_ref=recv.at[c, group, rest, span],
                send_sem=far_send, recv_sem=far_recv.at[k],
                device_id=at(peer, position), device_id_type=MESH,
            ).start()
            return carry

        lax.fori_loop(1, far, one, 0)

    def arrive_near(k):
        c, first, count = parts[k]
        span = pl.ds(first * unit, count * unit)
        slots = stage.at[c, :, pl.ds(1, NEAR - 1), span]
        pltpu.make_async_copy(slots, slots, near_recv.at[k]).wait()
        recv[c, group, 1:, span] = stage[c, group, 1:, span]

    spectra(0)
    pl.semaphore_wait(barrier, NEAR + far - 1)

    ship_near(0)
    ship_own(0)
    ship_near(1)
    ship_own(1)
    for load in loads[1 + chunks :]:
        load.start()
    for j in range(1, NEAR):
        pltpu.make_async_remote_copy(
            src_ref=near_buf.at[:, position], dst_ref=near_buf.at[:, position],
            send_sem=dark_near_sem.at[0], recv_sem=dark_near_sem.at[1],
            device_id=at(group, near_peer(j)), device_id_type=MESH,
        ).start()
    for c in range(1, chunks):
        spectra(c)
        for k, part in enumerate(parts):
            if part[0] == c:
                ship_own(k)

    small[1].wait()
    turned = jnp.concatenate([exposure[...], jnp.zeros_like(exposure[...])], axis=0).T
    for y in range(rows):
        rest = jnp.broadcast_to(turned[:, y : y + 1], (nx, LANES))
        total = jnp.zeros((2 * nx, LANES), jnp.float32)
        for _ in range(3):
            high = rest.astype(jnp.bfloat16)
            total += jnp.dot(row_v[...], high, preferred_element_type=jnp.float32)
            rest = rest - high.astype(jnp.float32)
        wide[pl.ds(y, 2 * nx, stride=rows), :] = total
    per_row = LANES // q_rows
    per_group = NEAR // per_row
    diagonal = lax.broadcasted_iota(jnp.int32, (LANES, LANES), 0) == lax.broadcasted_iota(
        jnp.int32, (LANES, LANES), 1
    )

    def pack(g, carry):
        for h in range(per_group):
            start = pl.multiple_of((g * per_group + h) * LANES, LANES)
            row = jnp.where(diagonal, wide[pl.ds(start, LANES)], 0.0)
            level_out[h, pl.ds(g, 1)] = jnp.sum(row, axis=0, keepdims=True)
        return carry

    lax.fori_loop(0, far, pack, 0)
    half = lax.div(position, per_row)
    level_stage[0] = level_out[half]
    for j in range(1, NEAR):
        peer = near_peer(j)
        pltpu.make_async_remote_copy(
            src_ref=level_out.at[lax.div(peer, per_row)], dst_ref=level_stage.at[NEAR - j],
            send_sem=level_near_sem.at[0], recv_sem=level_near_sem.at[1],
            device_id=at(group, peer), device_id_type=MESH,
        ).start()
    for k in range(2, len(parts)):
        ship_near(k)

    arrive_near(0)
    ship_far(0)
    arrive_near(1)
    ship_far(1)

    near_some = near_buf.at[:, pl.ds(0, NEAR - 1)]
    pltpu.make_async_copy(near_some, near_some, dark_near_sem.at[1]).wait()
    far_buf[group] = jnp.sum(near_buf[lax.rem(position, chunks)], axis=0)

    def send_dark(j, carry):
        pltpu.make_async_remote_copy(
            src_ref=far_buf.at[group], dst_ref=far_buf.at[group],
            send_sem=dark_far_sem.at[0], recv_sem=dark_far_sem.at[1],
            device_id=at(far_peer(j), position), device_id_type=MESH,
        ).start()
        return carry

    lax.fori_loop(1, far, send_dark, 0)


    level_near = level_stage.at[pl.ds(1, NEAR - 1)]
    pltpu.make_async_copy(level_near, level_near, level_near_sem.at[1]).wait()
    lane = lax.broadcasted_iota(jnp.int32, (far, LANES), 1)
    place = lax.rem(position, per_row)
    for h in range(per_group):
        row = jnp.zeros((far, LANES), jnp.float32)
        for m in range(per_row):
            block = jnp.where(lane // q_rows == place, level_stage[h * per_row + m], 0.0)
            row += pltpu.roll(block, lax.rem((m - place + per_row) * q_rows, LANES), axis=1)
        level_pack[h] = row.reshape(far, 1, LANES)
    level_in[:, group] = level_pack[:, group]

    def send_level(j, carry):
        peer = far_peer(j)
        pltpu.make_async_remote_copy(
            src_ref=level_pack.at[:, peer], dst_ref=level_in.at[:, group],
            send_sem=level_far_sem.at[0], recv_sem=level_far_sem.at[1],
            device_id=at(peer, position), device_id_type=MESH,
        ).start()
        return carry

    lax.fori_loop(1, far, send_level, 0)

    for k in range(2, len(parts)):
        arrive_near(k)
        ship_far(k)

    small[2].wait()
    angle = jnp.broadcast_to(aberration[...], (8, aberration.shape[1]))
    cos, sin = jnp.cos(angle), jnp.sin(angle)
    for c in range(chunks):
        turn[c, 0] = cos[:, c * LANES : (c + 1) * LANES]
        turn[c, 1] = sin[:, c * LANES : (c + 1) * LANES]
    acc[...] = jnp.zeros_like(acc)
    level_far = level_in.at[:, pl.ds(0, far - 1)]
    pltpu.make_async_copy(level_far, level_far, level_far_sem.at[1]).wait()
    columns = level_in[...].reshape(per_group * far, LANES).T
    index = lax.broadcasted_iota(jnp.int32, (q_rows, per_group * far), 1)

    def unpack(g, carry):
        for h in range(per_group):
            for m in range(per_row):
                block = jnp.where(index == h * far + g, columns[m * q_rows : (m + 1) * q_rows], 0.0)
                level[g, h * per_row + m] = jnp.broadcast_to(
                    jnp.sum(block, axis=1, keepdims=True), (q_rows, LANES)
                )
        return carry

    lax.fori_loop(0, far, unpack, 0)
    far_some = far_buf.at[pl.ds(0, far - 1)]
    pltpu.make_async_copy(far_some, far_some, dark_far_sem.at[1]).wait()
    dark_row[position] = jnp.sum(far_buf[...], axis=0) / frame_total
    for j in range(1, NEAR):
        pltpu.make_async_remote_copy(
            src_ref=dark_row.at[position], dst_ref=dark_row.at[position],
            send_sem=dark_row_sem.at[0], recv_sem=dark_row_sem.at[1],
            device_id=at(group, near_peer(j)), device_id_type=MESH,
        ).start()
    rows_some = dark_row.at[pl.ds(0, NEAR - 1)]
    pltpu.make_async_copy(rows_some, rows_some, dark_row_sem.at[1]).wait()

    loads[1 + chunks].wait()

    def weigh(k):
        c, first, count = parts[k]
        if first == 0:
            loads[2 + chunks + c].wait()
        span = pl.ds(first * unit, count * unit)
        others = recv.at[c, pl.ds(0, far - 1), :, span]
        pltpu.make_async_copy(others, others, far_recv.at[k]).wait()
        dark_mean = jnp.broadcast_to(dark_row[c], (count * unit, LANES))

        def regroup(g, carry):
            for m in range(NEAR // 2):
                blocks = []
                for source in (2 * m, 2 * m + 1):
                    slot = lax.rem(source - position + NEAR, NEAR)
                    block = recv[c, g, slot, span].astype(jnp.float32)
                    blocks.append(block - level[g, slot, span] * dark_mean)
                to = pl.ds(pl.multiple_of((g * NEAR + 2 * m) * unit, 2 * unit), 2 * unit)
                for q in range(count):
                    pair = [block[q * unit : (q + 1) * unit] for block in blocks]
                    gathered[to, q * LANES : (q + 1) * LANES] = jnp.concatenate(
                        pair, axis=0
                    ).astype(jnp.bfloat16)
            return carry

        lax.fori_loop(0, far, regroup, 0)
        cos = jnp.broadcast_to(turn[c, 0, 0:1], (tile, LANES))
        sin = jnp.broadcast_to(turn[c, 1, 0:1], (tile, LANES))

        def column(t, carry):
            full = jnp.dot(
                col_v[t], gathered[:, : count * LANES], preferred_element_type=jnp.float32
            )
            here = pl.ds(pl.multiple_of(t * tile, tile), tile)
            for q in range(count):
                real = full[:tile, q * LANES : (q + 1) * LANES]
                imag = full[tile:, q * LANES : (q + 1) * LANES]
                code = codes_v[c, first + q, here]
                weight = (code == 1).astype(jnp.float32) - (code == 2).astype(jnp.float32)
                acc[first + q, here] += weight * (real * cos + imag * sin)
                acc[rows + first + q, here] += weight * (imag * cos - real * sin)
            return carry

        lax.fori_loop(0, col_v.shape[0], column, 0)

    row = lax.broadcasted_iota(jnp.int32, (2 * rows, LANES), 0)

    def lane_sum(total, first, count):
        for i in [p * rows + first + q for p in range(2) for q in range(count)]:
            pick = (row == i).astype(jnp.bfloat16)
            value = acc[i]
            for _ in range(2):
                high = value.astype(jnp.bfloat16)
                total += lax.dot_general(
                    pick, high, (((1,), (1,)), ((), ())), preferred_element_type=jnp.float32
                )
                value = value - high.astype(jnp.float32)
        return total

    total = jnp.zeros((2 * rows, acc.shape[1]), jnp.float32)
    for k, (c, first, count) in enumerate(parts):
        weigh(k)
        if c == chunks - 1:
            total = lane_sum(total, first, count)
    total = total / scale
    width = half_in.shape[1]
    halves[0] = total[:, :width]
    halves[1] = total[:, width:]
    swap = pltpu.make_async_remote_copy(
        src_ref=halves.at[1 - det], dst_ref=half_in, send_sem=det_sem.at[0],
        recv_sem=det_sem.at[1], device_id={"det": 1 - det}, device_id_type=MESH,
    )
    swap.start()

    pltpu.make_async_copy(near_some, near_some, dark_near_sem.at[0]).wait()
    pltpu.make_async_copy(rows_some, rows_some, dark_row_sem.at[0]).wait()
    pltpu.make_async_copy(far_some, far_some, dark_far_sem.at[0]).wait()
    pltpu.make_async_copy(level_near, level_near, level_near_sem.at[0]).wait()
    pltpu.make_async_copy(level_far, level_far, level_far_sem.at[0]).wait()
    slots = stage.at[:, :, pl.ds(1, NEAR - 1)]
    pltpu.make_async_copy(slots, slots, near_send).wait()
    others = recv.at[:, pl.ds(0, far - 1)]
    pltpu.make_async_copy(others, others, far_send).wait()

    swap.wait()
    result = halves[det] + half_in[...]
    out[0] = result[:rows]
    out[1] = result[rows:]


def solution(mesh):
    n = mesh.shape["scan"]

    def on_device(frames, exposure, dark_counts, aberration, margin_codes):
        rows, nx, pix = frames.shape
        ny = rows * n
        chunks = pix // LANES
        tile = 256
        far = n // NEAR
        q_rows = 2 * rows * rows
        row_tab = row_table(nx)
        col_tab = column_table(ny, rows, tile)
        hbm = pl.BlockSpec(memory_space=pl.ANY)
        vmem = pl.BlockSpec(memory_space=pltpu.VMEM)
        body = functools.partial(
            kernel, n, rows, chunks, tile, dark_counts.shape[0] * n,
            math.sqrt(pix * mesh.shape["det"]),
        )
        spectra = pltpu.VMEM((chunks, far, NEAR, q_rows, LANES), jnp.bfloat16)
        packed = pltpu.VMEM((NEAR * q_rows // LANES, far, 1, LANES), jnp.float32)
        return pl.pallas_call(
            body,
            out_shape=jax.ShapeDtypeStruct((2, rows, ny // mesh.shape["det"]), jnp.float32),
            in_specs=[hbm] * 7,
            out_specs=vmem,
            scratch_shapes=[
                pltpu.VMEM((rows, nx), jnp.float32),
                pltpu.VMEM(dark_counts.shape, jnp.int32),
                pltpu.VMEM((1, pix), jnp.float32),
                pltpu.VMEM((chunks, rows, nx, LANES), jnp.bfloat16),
                pltpu.VMEM((chunks, rows, ny, LANES), jnp.int32),
                pltpu.VMEM(row_tab.shape, jnp.bfloat16),
                pltpu.VMEM(col_tab.shape, jnp.bfloat16),
                pltpu.VMEM((nx, rows * LANES), jnp.bfloat16),
                pltpu.VMEM((n * q_rows, LANES), jnp.float32),
                pltpu.VMEM((far, NEAR, q_rows, LANES), jnp.float32),
                spectra,
                spectra,
                spectra,
                pltpu.VMEM((2 * ny, rows * LANES), jnp.bfloat16),
                pltpu.VMEM((2 * rows, ny, LANES), jnp.float32),
                pltpu.VMEM((chunks, NEAR, 1, LANES), jnp.float32),
                pltpu.VMEM((far, 1, LANES), jnp.float32),
                pltpu.VMEM((NEAR, 1, LANES), jnp.float32),
                pltpu.VMEM((chunks, 2, 8, LANES), jnp.float32),
                pltpu.VMEM((NEAR * q_rows // LANES, far, LANES), jnp.float32),
                pltpu.VMEM((NEAR, far, LANES), jnp.float32),
                packed,
                packed,
                pltpu.VMEM((2, 2 * rows, ny // 2), jnp.float32),
                pltpu.VMEM((2 * rows, ny // 2), jnp.float32),
                pltpu.SemaphoreType.DMA((3,)),
                pltpu.SemaphoreType.DMA((2 + 2 * chunks,)),
                pltpu.SemaphoreType.DMA((2,)),
                pltpu.SemaphoreType.DMA((2,)),
                pltpu.SemaphoreType.DMA((2,)),
                pltpu.SemaphoreType.DMA((2,)),
                pltpu.SemaphoreType.DMA((2,)),
                pltpu.SemaphoreType.DMA,
                pltpu.SemaphoreType.DMA((chunks + 2,)),
                pltpu.SemaphoreType.DMA,
                pltpu.SemaphoreType.DMA((chunks + 2,)),
                pltpu.SemaphoreType.DMA((2,)),
            ],
            compiler_params=pltpu.CompilerParams(
                collective_id=0, has_side_effects=True, vmem_limit_bytes=63 * 1024 * 1024
            ),
        )(
            frames, exposure, dark_counts, aberration.reshape(1, pix), margin_codes,
            jnp.asarray(row_tab), jnp.asarray(col_tab),
        )

    placed = (
        P("scan", None, "det"),
        P("scan", None),
        P("scan", "det"),
        P("det"),
        P("scan", None, "det"),
    )
    return jax.shard_map(
        on_device, mesh=mesh, in_specs=placed, out_specs=P(None, "scan", "det"), check_vma=False
    )
```

```python
import functools
import math

import jax
import jax.numpy as jnp
import ml_dtypes
import numpy as np
from jax import lax
from jax.experimental import pallas as pl
from jax.experimental.pallas import tpu as pltpu
from jax.sharding import PartitionSpec as P

MESH = pl.DeviceIdType.MESH
LANES = 128
NEAR = 8


def dft_tables(length):
    index_row = np.arange(length, dtype=np.int64)
    products = (index_row[:, None] * index_row[None, :] % length).astype(np.float32)
    phase = np.float32(2.0 * math.pi / length) * products
    scale = np.float32(1.0 / math.sqrt(length))
    return (
        (np.cos(phase) * scale).astype(ml_dtypes.bfloat16),
        (-np.sin(phase) * scale).astype(ml_dtypes.bfloat16),
    )


def row_table(length):
    cos, sin = dft_tables(length)
    return np.stack([cos.T, sin.T], axis=1).reshape(2 * length, length)


def column_table(length, rows, tile):
    cos, sin = dft_tables(length)
    real = np.stack([cos, -sin], axis=1)
    imag = np.stack([sin, cos], axis=1)
    both = np.stack([real, imag]).reshape(2, length, 2, length // rows, rows)
    both = both.transpose(0, 1, 3, 2, 4).reshape(2, length // tile, tile, 2 * length)
    return np.ascontiguousarray(both.transpose(1, 0, 2, 3)).reshape(
        length // tile, 2 * tile, 2 * length
    )


def kernel(
    n, rows, chunks, tile, frame_total, scale,
    frames, exposure_h, dark_h, aberration_h, codes, row_tab, col_tab, out,
    exposure, dark, aberration,
    frames_v, codes_v, row_v, col_v, joined, wide, level, send, stage, recv, gathered, acc,
    near_buf, far_buf, dark_row, turn, level_out, level_stage, level_pack, level_in, halves, half_in,
    small_sem, load_sem, dark_near_sem, dark_far_sem, dark_row_sem, level_near_sem, level_far_sem,
    near_send, near_recv, far_send, far_recv, det_sem,
):
    me = lax.axis_index("scan")
    det = lax.axis_index("det")
    nx = frames_v.shape[2]
    unit = 2 * rows
    q_rows = unit * rows
    far = n // NEAR
    position = lax.rem(me, NEAR)
    group = lax.div(me, NEAR)

    def near_peer(j):
        return lax.rem(position + j, NEAR)

    cross = (group >> 2) & 1

    def far_peer(j):
        step = jnp.int32(j) - 1
        first = step < 7 + cross
        high = jnp.where(first, cross, 1 - cross)
        base = jnp.where(first, step + 1 - cross, step - 7)
        return group ^ ((base & 3) | ((base & 4) << 1) | (high << 2))

    def at(g, p):
        return {"scan": g * NEAR + p}

    barrier = pltpu.get_barrier_semaphore()
    for j in range(1, far):
        pl.semaphore_signal(
            barrier, inc=1, device_id=at(far_peer(j), position), device_id_type=MESH
        )
    for j in range(1, NEAR):
        pl.semaphore_signal(barrier, inc=1, device_id=at(group, near_peer(j)), device_id_type=MESH)
    pl.semaphore_signal(barrier, inc=1, device_id={"det": 1 - det}, device_id_type=MESH)

    small = [
        pltpu.make_async_copy(dark_h, dark, small_sem.at[0]),
        pltpu.make_async_copy(exposure_h, exposure, small_sem.at[1]),
        pltpu.make_async_copy(aberration_h, aberration, small_sem.at[2]),
    ]
    loads = [pltpu.make_async_copy(row_tab, row_v, load_sem.at[0])]
    loads += [
        pltpu.make_async_copy(
            frames.at[:, :, pl.ds(c * LANES, LANES)], frames_v.at[c], load_sem.at[1 + c]
        )
        for c in range(chunks)
    ]
    loads.append(pltpu.make_async_copy(col_tab, col_v, load_sem.at[1 + chunks]))
    loads += [
        pltpu.make_async_copy(
            codes.at[:, :, pl.ds(c * LANES, LANES)], codes_v.at[c], load_sem.at[2 + chunks + c]
        )
        for c in range(chunks)
    ]
    first_loads = small + loads[: 1 + chunks]
    for load in first_loads:
        load.start()

    small[0].wait()
    counted = jnp.sum(dark[...].astype(jnp.float32), axis=0, keepdims=True)
    for c in range(chunks):
        near_buf[c, position] = counted[:, c * LANES : (c + 1) * LANES]
    loads[0].wait()
    m_tile = 512

    parts = []
    for c in range(chunks):
        count = rows // 2
        parts += [(c, first, count) for first in range(0, rows, count)]

    def spectra(c):
        loads[1 + c].wait()
        for y in range(rows):
            joined[:, y * LANES : (y + 1) * LANES] = frames_v[c, y]
        for m in range(2 * nx // m_tile):
            part = jnp.dot(
                row_v[m * m_tile : (m + 1) * m_tile], joined[...],
                preferred_element_type=jnp.float32,
            )
            for y in range(rows):
                wide[pl.ds(m * m_tile * rows + y, m_tile, stride=rows), :] = part[
                    :, y * LANES : (y + 1) * LANES
                ]

        def narrow(g, carry):
            block = wide[pl.ds(pl.multiple_of(g * NEAR * q_rows, q_rows), NEAR * q_rows)]
            send[c, g] = block.astype(jnp.bfloat16).reshape(NEAR, q_rows, LANES)
            return carry

        lax.fori_loop(0, far, narrow, 0)
        recv[c, group, 0] = send[c, group, position]

    def ship_near(k):
        c, first, count = parts[k]
        span = pl.ds(first * unit, count * unit)
        for j in range(1, NEAR):
            peer = near_peer(j)
            pltpu.make_async_remote_copy(
                src_ref=send.at[c, :, peer, span], dst_ref=stage.at[c, :, NEAR - j, span],
                send_sem=near_send, recv_sem=near_recv.at[k],
                device_id=at(group, peer), device_id_type=MESH,
            ).start()

    def ship_own(k):
        c, first, count = parts[k]
        span = pl.ds(first * unit, count * unit)

        def one(j, carry):
            peer = far_peer(j)
            pltpu.make_async_remote_copy(
                src_ref=send.at[c, peer, position, span], dst_ref=recv.at[c, group, 0, span],
                send_sem=far_send, recv_sem=far_recv.at[k],
                device_id=at(peer, position), device_id_type=MESH,
            ).start()
            return carry

        lax.fori_loop(1, far, one, 0)

    def ship_far(k):
        c, first, count = parts[k]
        span = pl.ds(first * unit, count * unit)
        rest = pl.ds(1, NEAR - 1)

        def one(j, carry):
            peer = far_peer(j)
            pltpu.make_async_remote_copy(
                src_ref=stage.at[c, peer, rest, span], dst_ref=recv.at[c, group, rest, span],
                send_sem=far_send, recv_sem=far_recv.at[k],
                device_id=at(peer, position), device_id_type=MESH,
            ).start()
            return carry

        lax.fori_loop(1, far, one, 0)

    def arrive_near(k):
        c, first, count = parts[k]
        span = pl.ds(first * unit, count * unit)
        slots = stage.at[c, :, pl.ds(1, NEAR - 1), span]
        pltpu.make_async_copy(slots, slots, near_recv.at[k]).wait()
        recv[c, group, 1:, span] = stage[c, group, 1:, span]

    spectra(0)
    pl.semaphore_wait(barrier, NEAR + far - 1)

    ship_near(0)
    ship_own(0)
    ship_near(1)
    ship_own(1)
    for load in loads[1 + chunks :]:
        load.start()
    for j in range(1, NEAR):
        pltpu.make_async_remote_copy(
            src_ref=near_buf.at[:, position], dst_ref=near_buf.at[:, position],
            send_sem=dark_near_sem.at[0], recv_sem=dark_near_sem.at[1],
            device_id=at(group, near_peer(j)), device_id_type=MESH,
        ).start()
    for c in range(1, chunks):
        spectra(c)
        for k, part in enumerate(parts):
            if part[0] == c:
                ship_own(k)

    small[1].wait()
    turned = jnp.concatenate([exposure[...], jnp.zeros_like(exposure[...])], axis=0).T
    for y in range(rows):
        rest = jnp.broadcast_to(turned[:, y : y + 1], (nx, LANES))
        total = jnp.zeros((2 * nx, LANES), jnp.float32)
        for _ in range(3):
            high = rest.astype(jnp.bfloat16)
            total += jnp.dot(row_v[...], high, preferred_element_type=jnp.float32)
            rest = rest - high.astype(jnp.float32)
        wide[pl.ds(y, 2 * nx, stride=rows), :] = total
    per_row = LANES // q_rows
    per_group = NEAR // per_row
    diagonal = lax.broadcasted_iota(jnp.int32, (LANES, LANES), 0) == lax.broadcasted_iota(
        jnp.int32, (LANES, LANES), 1
    )

    def pack(g, carry):
        for h in range(per_group):
            start = pl.multiple_of((g * per_group + h) * LANES, LANES)
            row = jnp.where(diagonal, wide[pl.ds(start, LANES)], 0.0)
            level_out[h, pl.ds(g, 1)] = jnp.sum(row, axis=0, keepdims=True)
        return carry

    lax.fori_loop(0, far, pack, 0)
    half = lax.div(position, per_row)
    level_stage[0] = level_out[half]
    for j in range(1, NEAR):
        peer = near_peer(j)
        pltpu.make_async_remote_copy(
            src_ref=level_out.at[lax.div(peer, per_row)], dst_ref=level_stage.at[NEAR - j],
            send_sem=level_near_sem.at[0], recv_sem=level_near_sem.at[1],
            device_id=at(group, peer), device_id_type=MESH,
        ).start()
    for k in range(2, len(parts)):
        ship_near(k)

    arrive_near(0)
    ship_far(0)
    arrive_near(1)
    ship_far(1)

    near_some = near_buf.at[:, pl.ds(0, NEAR - 1)]
    pltpu.make_async_copy(near_some, near_some, dark_near_sem.at[1]).wait()
    far_buf[group] = jnp.sum(near_buf[lax.rem(position, chunks)], axis=0)

    def send_dark(j, carry):
        pltpu.make_async_remote_copy(
            src_ref=far_buf.at[group], dst_ref=far_buf.at[group],
            send_sem=dark_far_sem.at[0], recv_sem=dark_far_sem.at[1],
            device_id=at(far_peer(j), position), device_id_type=MESH,
        ).start()
        return carry

    lax.fori_loop(1, far, send_dark, 0)


    level_near = level_stage.at[pl.ds(1, NEAR - 1)]
    pltpu.make_async_copy(level_near, level_near, level_near_sem.at[1]).wait()
    lane = lax.broadcasted_iota(jnp.int32, (far, LANES), 1)
    place = lax.rem(position, per_row)
    for h in range(per_group):
        row = jnp.zeros((far, LANES), jnp.float32)
        for m in range(per_row):
            block = jnp.where(lane // q_rows == place, level_stage[h * per_row + m], 0.0)
            row += pltpu.roll(block, lax.rem((m - place + per_row) * q_rows, LANES), axis=1)
        level_pack[h] = row.reshape(far, 1, LANES)
    level_in[:, group] = level_pack[:, group]

    def send_level(j, carry):
        peer = far_peer(j)
        pltpu.make_async_remote_copy(
            src_ref=level_pack.at[:, peer], dst_ref=level_in.at[:, group],
            send_sem=level_far_sem.at[0], recv_sem=level_far_sem.at[1],
            device_id=at(peer, position), device_id_type=MESH,
        ).start()
        return carry

    lax.fori_loop(1, far, send_level, 0)

    for k in range(2, len(parts)):
        arrive_near(k)
        ship_far(k)

    small[2].wait()
    angle = jnp.broadcast_to(aberration[...], (8, aberration.shape[1]))
    cos, sin = jnp.cos(angle), jnp.sin(angle)
    for c in range(chunks):
        turn[c, 0] = cos[:, c * LANES : (c + 1) * LANES]
        turn[c, 1] = sin[:, c * LANES : (c + 1) * LANES]
    acc[...] = jnp.zeros_like(acc)
    level_far = level_in.at[:, pl.ds(0, far - 1)]
    pltpu.make_async_copy(level_far, level_far, level_far_sem.at[1]).wait()
    columns = level_in[...].reshape(per_group * far, LANES).T
    index = lax.broadcasted_iota(jnp.int32, (q_rows, per_group * far), 1)

    def unpack(g, carry):
        for h in range(per_group):
            for m in range(per_row):
                block = jnp.where(index == h * far + g, columns[m * q_rows : (m + 1) * q_rows], 0.0)
                level[g, h * per_row + m] = jnp.broadcast_to(
                    jnp.sum(block, axis=1, keepdims=True), (q_rows, LANES)
                )
        return carry

    lax.fori_loop(0, far, unpack, 0)
    far_some = far_buf.at[pl.ds(0, far - 1)]
    pltpu.make_async_copy(far_some, far_some, dark_far_sem.at[1]).wait()
    dark_row[position] = jnp.sum(far_buf[...], axis=0) / frame_total
    for j in range(1, NEAR):
        pltpu.make_async_remote_copy(
            src_ref=dark_row.at[position], dst_ref=dark_row.at[position],
            send_sem=dark_row_sem.at[0], recv_sem=dark_row_sem.at[1],
            device_id=at(group, near_peer(j)), device_id_type=MESH,
        ).start()
    rows_some = dark_row.at[pl.ds(0, NEAR - 1)]
    pltpu.make_async_copy(rows_some, rows_some, dark_row_sem.at[1]).wait()

    loads[1 + chunks].wait()

    def weigh(k):
        c, first, count = parts[k]
        if first == 0:
            loads[2 + chunks + c].wait()
        span = pl.ds(first * unit, count * unit)
        others = recv.at[c, pl.ds(0, far - 1), :, span]
        pltpu.make_async_copy(others, others, far_recv.at[k]).wait()
        dark_mean = jnp.broadcast_to(dark_row[c], (count * unit, LANES))

        def regroup(g, carry):
            for m in range(NEAR // 2):
                blocks = []
                for source in (2 * m, 2 * m + 1):
                    slot = lax.rem(source - position + NEAR, NEAR)
                    block = recv[c, g, slot, span].astype(jnp.float32)
                    blocks.append(block - level[g, slot, span] * dark_mean)
                to = pl.ds(pl.multiple_of((g * NEAR + 2 * m) * unit, 2 * unit), 2 * unit)
                for q in range(count):
                    pair = [block[q * unit : (q + 1) * unit] for block in blocks]
                    gathered[to, q * LANES : (q + 1) * LANES] = jnp.concatenate(
                        pair, axis=0
                    ).astype(jnp.bfloat16)
            return carry

        lax.fori_loop(0, far, regroup, 0)
        cos = jnp.broadcast_to(turn[c, 0, 0:1], (tile, LANES))
        sin = jnp.broadcast_to(turn[c, 1, 0:1], (tile, LANES))

        def column(t, carry):
            full = jnp.dot(
                col_v[t], gathered[:, : count * LANES], preferred_element_type=jnp.float32
            )
            here = pl.ds(pl.multiple_of(t * tile, tile), tile)
            for q in range(count):
                real = full[:tile, q * LANES : (q + 1) * LANES]
                imag = full[tile:, q * LANES : (q + 1) * LANES]
                code = codes_v[c, first + q, here]
                weight = (code == 1).astype(jnp.float32) - (code == 2).astype(jnp.float32)
                acc[first + q, here] += weight * (real * cos + imag * sin)
                acc[rows + first + q, here] += weight * (imag * cos - real * sin)
            return carry

        lax.fori_loop(0, col_v.shape[0], column, 0)

    row = lax.broadcasted_iota(jnp.int32, (2 * rows, LANES), 0)

    def lane_sum(total, first, count):
        for i in [p * rows + first + q for p in range(2) for q in range(count)]:
            pick = (row == i).astype(jnp.bfloat16)
            value = acc[i]
            for _ in range(2):
                high = value.astype(jnp.bfloat16)
                total += lax.dot_general(
                    pick, high, (((1,), (1,)), ((), ())), preferred_element_type=jnp.float32
                )
                value = value - high.astype(jnp.float32)
        return total

    total = jnp.zeros((2 * rows, acc.shape[1]), jnp.float32)
    for k, (c, first, count) in enumerate(parts):
        weigh(k)
        if c == chunks - 1:
            total = lane_sum(total, first, count)
    total = total / scale
    width = half_in.shape[1]
    halves[0] = total[:, :width]
    halves[1] = total[:, width:]
    swap = pltpu.make_async_remote_copy(
        src_ref=halves.at[1 - det], dst_ref=half_in, send_sem=det_sem.at[0],
        recv_sem=det_sem.at[1], device_id={"det": 1 - det}, device_id_type=MESH,
    )
    swap.start()

    pltpu.make_async_copy(near_some, near_some, dark_near_sem.at[0]).wait()
    pltpu.make_async_copy(rows_some, rows_some, dark_row_sem.at[0]).wait()
    pltpu.make_async_copy(far_some, far_some, dark_far_sem.at[0]).wait()
    pltpu.make_async_copy(level_near, level_near, level_near_sem.at[0]).wait()
    pltpu.make_async_copy(level_far, level_far, level_far_sem.at[0]).wait()
    slots = stage.at[:, :, pl.ds(1, NEAR - 1)]
    pltpu.make_async_copy(slots, slots, near_send).wait()
    others = recv.at[:, pl.ds(0, far - 1)]
    pltpu.make_async_copy(others, others, far_send).wait()

    swap.wait()
    result = halves[det] + half_in[...]
    out[0] = result[:rows]
    out[1] = result[rows:]


def solution(mesh):
    n = mesh.shape["scan"]

    def on_device(frames, exposure, dark_counts, aberration, margin_codes):
        rows, nx, pix = frames.shape
        ny = rows * n
        chunks = pix // LANES
        tile = 256
        far = n // NEAR
        q_rows = 2 * rows * rows
        row_tab = row_table(nx)
        col_tab = column_table(ny, rows, tile)
        hbm = pl.BlockSpec(memory_space=pl.ANY)
        vmem = pl.BlockSpec(memory_space=pltpu.VMEM)
        body = functools.partial(
            kernel, n, rows, chunks, tile, dark_counts.shape[0] * n,
            math.sqrt(pix * mesh.shape["det"]),
        )
        spectra = pltpu.VMEM((chunks, far, NEAR, q_rows, LANES), jnp.bfloat16)
        packed = pltpu.VMEM((NEAR * q_rows // LANES, far, 1, LANES), jnp.float32)
        return pl.pallas_call(
            body,
            out_shape=jax.ShapeDtypeStruct((2, rows, ny // mesh.shape["det"]), jnp.float32),
            in_specs=[hbm] * 7,
            out_specs=vmem,
            scratch_shapes=[
                pltpu.VMEM((rows, nx), jnp.float32),
                pltpu.VMEM(dark_counts.shape, jnp.int32),
                pltpu.VMEM((1, pix), jnp.float32),
                pltpu.VMEM((chunks, rows, nx, LANES), jnp.bfloat16),
                pltpu.VMEM((chunks, rows, ny, LANES), jnp.int32),
                pltpu.VMEM(row_tab.shape, jnp.bfloat16),
                pltpu.VMEM(col_tab.shape, jnp.bfloat16),
                pltpu.VMEM((nx, rows * LANES), jnp.bfloat16),
                pltpu.VMEM((n * q_rows, LANES), jnp.float32),
                pltpu.VMEM((far, NEAR, q_rows, LANES), jnp.float32),
                spectra,
                spectra,
                spectra,
                pltpu.VMEM((2 * ny, rows * LANES), jnp.bfloat16),
                pltpu.VMEM((2 * rows, ny, LANES), jnp.float32),
                pltpu.VMEM((chunks, NEAR, 1, LANES), jnp.float32),
                pltpu.VMEM((far, 1, LANES), jnp.float32),
                pltpu.VMEM((NEAR, 1, LANES), jnp.float32),
                pltpu.VMEM((chunks, 2, 8, LANES), jnp.float32),
                pltpu.VMEM((NEAR * q_rows // LANES, far, LANES), jnp.float32),
                pltpu.VMEM((NEAR, far, LANES), jnp.float32),
                packed,
                packed,
                pltpu.VMEM((2, 2 * rows, ny // 2), jnp.float32),
                pltpu.VMEM((2 * rows, ny // 2), jnp.float32),
                pltpu.SemaphoreType.DMA((3,)),
                pltpu.SemaphoreType.DMA((2 + 2 * chunks,)),
                pltpu.SemaphoreType.DMA((2,)),
                pltpu.SemaphoreType.DMA((2,)),
                pltpu.SemaphoreType.DMA((2,)),
                pltpu.SemaphoreType.DMA((2,)),
                pltpu.SemaphoreType.DMA((2,)),
                pltpu.SemaphoreType.DMA,
                pltpu.SemaphoreType.DMA((2 * chunks,)),
                pltpu.SemaphoreType.DMA,
                pltpu.SemaphoreType.DMA((2 * chunks,)),
                pltpu.SemaphoreType.DMA((2,)),
            ],
            compiler_params=pltpu.CompilerParams(
                collective_id=0, has_side_effects=True, vmem_limit_bytes=63 * 1024 * 1024
            ),
        )(
            frames, exposure, dark_counts, aberration.reshape(1, pix), margin_codes,
            jnp.asarray(row_tab), jnp.asarray(col_tab),
        )

    placed = (
        P("scan", None, "det"),
        P("scan", None),
        P("scan", "det"),
        P("det"),
        P("scan", None, "det"),
    )
    return jax.shard_map(
        on_device, mesh=mesh, in_specs=placed, out_specs=P(None, "scan", "det"), check_vma=False
    )
```
